128 devices in a mesh: frame: 8 (over z_lo, x), row: 16 (over z_hi, y, core).
Axes of the slice: x: 4, y: 4, z: 4 (z_hi: 2, z_lo: 2; z = z_hi * 2 + z_lo), core: 2. Of those that a mesh axis runs over, the one named last changes fastest.
Arguments:
- base_latent: bfloat16 [8, 64, 8, 3072], P(None, 'row', 'frame'), may hold values from -6 to 6
- degraded: bfloat16 [8, 128, 16, 3072], P('frame', 'row'), may hold values from -6 to 6
- row_window: int32 [128], replicated, may hold values from 0 to 23, as said below
- column_shift: int32 [1], replicated, may hold values from 0 to 7
- norm_gain: float32 [3072], replicated, may hold values from 0.1 to 1.9
- project_in: bfloat16 [3072, 3, 3072], P(None, None, 'frame'), may hold values from -4 to 4
- project_out: bfloat16 [3072, 3072], P('frame'), may hold values from -1.75 to 1.75
Outputs:
- restored: bfloat16 [8, 128, 16, 3072], P('frame', 'row')
The draws below stay inside these ranges and needn't reach their ends.
Inputs may be any that keep to these rules, and one draw needn't show every extreme that they name: `row_window`: window numbers start at 0 and rise by one from a window to the next along the rows; each window has 1 to 8 rows, some have exactly 8, and there are 24 windows.
All inputs are finite; a program needn't handle non-finite values.
Results may differ from the reference program's by a relative error of at most 0.023.
Values may be sent and summed in bfloat16 or wider, within the bound.
A program may use at most 128 MiB of HBM per device.

```python
import jax
import jax.numpy as jnp
from jax import lax

HEAD = 128
D = 3072
ROWS_DEV = 8
COLS = 16
WIN_COLS = 8
FRAMES = 8
H = 128
N_FRAME = 8
N_ROW = 16


def draw_degraded(key, part):
    key = jax.random.fold_in(key, 11)
    shape = (FRAMES, H, COLS, D)
    values = jax.random.truncated_normal(key, -6.0, 6.0, shape, jnp.float32)
    return values.astype(jnp.bfloat16)


def draw_row_window(key, part):
    key = jax.random.fold_in(key, 37)
    key_side, key_pick, key_cut = jax.random.split(key, 3)
    band_count = H // ROWS_DEV
    full_count = band_count - 1
    split_count = full_count // 2
    side = jax.random.randint(key_side, (), 0, 2, jnp.int32)
    start_row = jnp.where(side == 0, 1, ROWS_DEV - 1).astype(jnp.int32)
    order = jax.random.permutation(key_pick, full_count)
    split_flag = jnp.zeros((full_count,), jnp.int32).at[order[:split_count]].set(1)
    cut_at = jax.random.randint(key_cut, (full_count,), 1, ROWS_DEV, jnp.int32)
    rows = jnp.arange(H, dtype=jnp.int32)
    relative = rows - start_row
    block = jnp.floor_divide(relative, ROWS_DEV)
    inner = relative - block * ROWS_DEV
    is_full = (block >= 0) & (block < full_count)
    safe_block = jnp.clip(block, 0, full_count - 1)
    opens = (inner == 0) & (block >= 0)
    splits = is_full & (split_flag[safe_block] == 1) & (inner == cut_at[safe_block])
    starts = (opens | splits).astype(jnp.int32)
    return jnp.cumsum(starts).astype(jnp.int32)


def draw_project_in(key, part):
    key = jax.random.fold_in(key, 23)
    key_base = jax.random.fold_in(key, 0)
    values = jax.random.truncated_normal(key_base, -6.0, 6.0, (D, 3, D), jnp.float32) * D ** (-0.5)
    return values.astype(jnp.bfloat16)


def level_of(key, shape, shards, low, top_value):
    gain = 1.0
    for position, shards_of in shards:
        steps = jax.random.uniform(jax.random.fold_in(jax.random.fold_in(key, 6), position), (shards_of,), jnp.float32, low / len(shards), top_value / len(shards))
        gain = gain * jnp.repeat(jnp.exp(steps), shape[position] // shards_of).reshape((-1,) + (1,) * (len(shape) - 1 - position))
    return gain


def centred(stream_key, extent, width, limit, shards=(), kind=jnp.bfloat16):
    entries = jax.random.normal(stream_key, extent, jnp.float32) * width
    if len(shards) > 0:
        entries = level_of(stream_key, extent, shards, -0.22, 0.18) * entries
    return jnp.clip(entries, min=-limit, max=limit).astype(kind)


def setup_inputs(seed: int = 0) -> dict:
    arg_keys = jax.random.split(jax.random.key(seed), 8)
    base_latent = centred(arg_keys[0], (FRAMES, H // 2, COLS // 2, D), 1.0, 6.0, ((1, 16), (2, 8)))
    degraded = draw_degraded(jax.random.fold_in(arg_keys[7], 71), 0)
    row_window = draw_row_window(jax.random.fold_in(arg_keys[7], 71), 0)
    column_shift = jax.random.randint(arg_keys[3], (1,), 0, WIN_COLS).astype(jnp.int32)
    norm_gain = jnp.clip(1.0 + 0.18 * jax.random.normal(arg_keys[4], (D,), jnp.float32), 0.1, 1.9)
    project_in = draw_project_in(jax.random.fold_in(arg_keys[7], 71), 0)
    project_out = centred(arg_keys[6], (D, D), (max(1, D // 256)) ** -0.5, 1.75, ((0, 8),))
    return dict(base_latent=base_latent, degraded=degraded, row_window=row_window, column_shift=column_shift, norm_gain=norm_gain, project_in=project_in, project_out=project_out)


def rms_normed(values, norm_gain):
    widened = values.astype(jnp.float32)
    scale = lax.rsqrt(lax.optimization_barrier(jnp.mean(widened * widened, axis=-1, keepdims=True)) + 1e-06)
    return (widened * scale * norm_gain).astype(jnp.bfloat16)

def window_attention(query, keyval, query_ids, key_ids, offset):
    frame_count, row_count, column_count, feature_width = query.shape
    head_count = feature_width // HEAD
    windows = column_count // WIN_COLS
    key_rows = keyval.shape[1]
    query = jnp.roll(query, -offset, axis=2)
    keyval = jnp.roll(keyval, -offset, axis=2)
    query_blocks = query.reshape(frame_count, row_count, windows, WIN_COLS, head_count, HEAD)
    query_blocks = query_blocks.transpose(2, 4, 0, 1, 3, 5).reshape(windows * head_count, frame_count * row_count * WIN_COLS, HEAD)
    pair_blocks = keyval.reshape(frame_count, key_rows, windows, WIN_COLS, 2, head_count, HEAD)
    pair_blocks = pair_blocks.transpose(4, 2, 5, 0, 1, 3, 6).reshape(2, windows * head_count, frame_count * key_rows * WIN_COLS, HEAD)
    query_tokens = jnp.broadcast_to(query_ids[None, :, None], (frame_count, row_count, WIN_COLS)).reshape(-1)
    key_tokens = jnp.broadcast_to(key_ids[None, :, None], (frame_count, key_rows, WIN_COLS)).reshape(-1)
    allowed = (query_tokens[:, None] == key_tokens[None, :]) & (key_tokens[None, :] >= 0)

    def one_block(block_parts):
        query_block, key_block, value_block = block_parts
        scores = jnp.dot(query_block, key_block.T, preferred_element_type=jnp.float32) * HEAD ** (-0.5)
        scores = jnp.where(allowed, scores, -1e+30)
        highest = lax.optimization_barrier(jnp.max(scores, axis=-1, keepdims=True))
        raised = jnp.exp(scores - highest)
        weights = (raised / lax.optimization_barrier(jnp.sum(raised, axis=-1, keepdims=True))).astype(jnp.bfloat16)
        return jnp.dot(weights, value_block, preferred_element_type=jnp.float32).astype(jnp.bfloat16)
    results = lax.map(one_block, (query_blocks, pair_blocks[0], pair_blocks[1]))
    results = results.reshape(windows, head_count, frame_count, row_count, WIN_COLS, HEAD)
    results = results.transpose(2, 3, 0, 4, 1, 5).reshape(frame_count, row_count, column_count, feature_width)
    return jnp.roll(results, offset, axis=2)

def reference(base_latent, degraded, row_window, column_shift, norm_gain, project_in, project_out):
    upsampled = jnp.repeat(jnp.repeat(base_latent, 2, axis=1), 2, axis=2)
    mixed_tokens = (upsampled.astype(jnp.float32) + degraded.astype(jnp.float32)).astype(jnp.bfloat16)
    normed = rms_normed(mixed_tokens, norm_gain)
    padded = jnp.pad(normed, ((0, 0), (ROWS_DEV, ROWS_DEV), (0, 0), (0, 0)))
    padded_ids = jnp.pad(row_window, (ROWS_DEV, ROWS_DEV), constant_values=-1)
    offset = column_shift[0]
    group_width = D // N_FRAME
    out_groups = project_out.reshape(N_FRAME, group_width, D).astype(jnp.float32)
    in_matrix = project_in.reshape(D, 3 * D)

    def one_band(band_index):
        first_row = (band_index * ROWS_DEV).astype(jnp.int32)
        own_rows = lax.dynamic_slice_in_dim(mixed_tokens, first_row, ROWS_DEV, 1)
        own_normed = lax.dynamic_slice_in_dim(normed, first_row, ROWS_DEV, 1)
        rim_rows = lax.dynamic_slice_in_dim(padded, first_row, 3 * ROWS_DEV, 1)
        query_ids = lax.dynamic_slice_in_dim(padded_ids, first_row + ROWS_DEV, ROWS_DEV, 0)
        key_ids = lax.dynamic_slice_in_dim(padded_ids, first_row, 3 * ROWS_DEV, 0)
        query = jnp.dot(own_normed.reshape(-1, D), in_matrix[:, :D], preferred_element_type=jnp.float32).astype(jnp.bfloat16)
        query = query.reshape(FRAMES, ROWS_DEV, COLS, D)
        keyval = jnp.dot(rim_rows.reshape(-1, D), in_matrix[:, D:], preferred_element_type=jnp.float32).astype(jnp.bfloat16)
        keyval = keyval.reshape(FRAMES, 3 * ROWS_DEV, COLS, 2, D)
        attended = window_attention(query, keyval, query_ids, key_ids, offset)
        grouped = attended.reshape(FRAMES, ROWS_DEV, COLS, N_FRAME, group_width).astype(jnp.float32)
        partials = jnp.einsum('frcgk,gke->frcge', grouped, out_groups, precision=lax.Precision.HIGHEST)
        rounded = lax.optimization_barrier(partials.astype(jnp.bfloat16))
        summed = lax.optimization_barrier(jnp.sum(rounded.astype(jnp.float32), axis=3))
        return (summed + own_rows.astype(jnp.float32)).astype(jnp.bfloat16)
    bands = lax.map(one_band, jnp.arange(N_ROW, dtype=jnp.int32))
    return bands.transpose(1, 0, 2, 3, 4).reshape(FRAMES, H, COLS, D)
```

```python
import functools

import jax
import jax.numpy as jnp
from jax import lax
from jax.experimental import pallas as pl
from jax.experimental.pallas import tpu as pltpu
from jax.sharding import PartitionSpec as P

MESH = pl.DeviceIdType.MESH
HEAD = 128
D = 3072
TOK = 128
QTR = 32
WIDTH = 384
CHUNK = 768
N_FIRST = 2
BF = jnp.bfloat16
F32 = jnp.float32


def place():
    frame = lax.axis_index("frame")
    row = lax.axis_index("row")
    return frame // 4, frame % 4, row


def packed_columns(shift, shape, dim):
    token = lax.broadcasted_iota(jnp.int32, shape, dim)
    position = (token // 64) * 8 + token % 8
    column = position + shift
    column = jnp.where(column >= 16, column - 16, column)
    return (token // 8) % 8, column


def gather_kernel(
    base_ref, deg_ref, shift_ref, gain_ref, win_ref, wout_ref,
    mixed_ref, q_ref, kv_ref, wpair_ref,
    g, b, w, base_sem, x_send, z_send, g_recv, kv_send, kv_recv, w_sem, wo_sem,
):
    z, x, row = place()
    me = z * 4 + x
    other = (1 - z) * 4
    right, left, opp = lax.rem(x + 1, 4), lax.rem(x + 3, 4), lax.rem(x + 2, 4)
    mate = row + 1 - 2 * lax.rem(row, 2)
    far_row = lax.rem(row + 8, 16)

    copies = []
    for k in range(3):
        copy = pltpu.make_async_copy(win_ref.at[k], w.at[k], w_sem.at[k])
        copy.start()
        copies.append(copy)

    barrier = pltpu.get_barrier_semaphore()
    for step in range(1, 8):
        pl.semaphore_signal(
            barrier, inc=1, device_id=(lax.rem(me + step, 8), row), device_id_type=MESH
        )
    for target in ((me, mate), (other + x, far_row)):
        pl.semaphore_signal(barrier, inc=1, device_id=target, device_id_type=MESH)
    outer = row + 2 * lax.rem(row, 2) - 1
    has_outer = jnp.logical_and(outer >= 0, outer < 16)

    @pl.when(has_outer)
    def _():
        pl.semaphore_signal(barrier, inc=1, device_id=(me, outer), device_id_type=MESH)
        pl.semaphore_wait(barrier, 10)

    @pl.when(jnp.logical_not(has_outer))
    def _():
        pl.semaphore_wait(barrier, 9)

    sends = []

    def remote(src, dst, send, recv, target):
        copy = pltpu.make_async_remote_copy(
            src_ref=src, dst_ref=dst, send_sem=send, recv_sem=recv,
            device_id=target, device_id_type=MESH,
        )
        copy.start()
        return copy

    base_copies = []
    for step in range(1, 8):
        to = lax.rem(me + step, 8)
        base_copies.append(
            remote(base_ref.at[to], b.at[me], base_sem.at[0, step], base_sem.at[1, step], (to, row))
        )
    own_base = pltpu.make_async_copy(base_ref.at[me], b.at[me], base_sem.at[0, 0])
    own_base.start()

    half = WIDTH // 2
    core = lax.rem(row, 2)
    mine = pl.ds(pl.multiple_of(core * half, half), half)
    w_first = remote(
        wout_ref.at[mine], wpair_ref.at[mine], wo_sem.at[0], wo_sem.at[1], (other + x, far_row)
    )

    shift = shift_ref[0]
    rows_q, cols_q = packed_columns(shift, (TOK, TOK), 0)
    source = lax.broadcasted_iota(jnp.int32, (TOK, TOK), 1)
    pick_fine = (source == rows_q * 16 + cols_q).astype(F32).astype(BF)

    own_base.wait()
    for copy in base_copies:
        copy.wait()

    square = jnp.zeros((TOK, 1), F32)
    for c in range(4):
        lanes = slice(c * CHUNK, (c + 1) * CHUNK)
        pick_base = (source == (cols_q // 2) * 16 + c * 4 + rows_q // 2).astype(F32).astype(BF)
        total = jnp.dot(pick_fine, deg_ref[:, lanes], preferred_element_type=F32) + jnp.dot(
            pick_base, b[...].reshape(TOK, CHUNK), preferred_element_type=F32
        )
        total = total.astype(BF)
        mixed_ref[:, lanes] = total
        total = total.astype(F32)
        square = square + jnp.sum(total * total, axis=1, keepdims=True)
    scale = lax.rsqrt(square * (1.0 / D) + 1e-06)
    for c in range(4):
        lanes = slice(c * CHUNK, (c + 1) * CHUNK)
        normed = mixed_ref[:, lanes].astype(F32) * scale * gain_ref[:, lanes]
        g[me, :, :, lanes] = normed.astype(BF).reshape(4, QTR, CHUNK)

    def item(plane, column):
        return (z * 4 if plane == 0 else other) + column

    def x_push(direction, plane, column, t, forward):
        frame = item(plane, column)
        to = right if direction == 0 else left
        sends.append(
            remote(g.at[frame, t], g.at[frame, t], x_send.at[direction, plane, forward, t],
                   g_recv.at[frame, t], (z * 4 + to, row))
        )

    def z_push(slot, column, t):
        frame = item(0, column)
        sends.append(
            remote(g.at[frame, t], g.at[frame, t], z_send.at[slot, t],
                   g_recv.at[frame, t], (other + x, row))
        )

    def arrive(plane, column, t):
        frame = item(plane, column)
        pltpu.make_async_remote_copy(
            src_ref=g.at[frame, t], dst_ref=g.at[frame, t], send_sem=z_send.at[0, 0],
            recv_sem=g_recv.at[frame, t], device_id=(other + x, row), device_id_type=MESH,
        ).wait_recv()

    kv_up, kv_down = [], []

    def project(plane, column):
        frame = item(plane, column)
        tokens = g[frame].reshape(TOK, D)
        q_ref[frame] = jnp.dot(tokens, w[0], preferred_element_type=F32).astype(BF)
        kv_ref[1, frame, :, :WIDTH] = jnp.dot(tokens, w[1], preferred_element_type=F32).astype(BF)
        kv_ref[1, frame, :, WIDTH:] = jnp.dot(tokens, w[2], preferred_element_type=F32).astype(BF)
        n = len(kv_up)
        up = pltpu.make_async_remote_copy(
            src_ref=kv_ref.at[1, frame], dst_ref=kv_ref.at[0, frame], send_sem=kv_send.at[0, n],
            recv_sem=kv_recv.at[0, n], device_id=(me, row + 1), device_id_type=MESH,
        )
        down = pltpu.make_async_remote_copy(
            src_ref=kv_ref.at[1, frame], dst_ref=kv_ref.at[2, frame], send_sem=kv_send.at[1, n],
            recv_sem=kv_recv.at[1, n], device_id=(me, row - 1), device_id_type=MESH,
        )
        kv_up.append(up)
        kv_down.append(down)

        @pl.when(row < 15)
        def _():
            up.start()

        @pl.when(row > 0)
        def _():
            down.start()

    first = range(N_FIRST)
    late = range(N_FIRST, 4)
    for t in range(4):
        if t in first:
            z_push(0, x, t)
        x_push(0, 0, x, t, 0)
        x_push(1, 0, x, t, 0)
    for t in late:
        z_push(0, x, t)

    @pl.when(row == 0)
    def _():
        kv_ref[0] = jnp.zeros(kv_ref.shape[1:], BF)

    @pl.when(row == 15)
    def _():
        kv_ref[2] = jnp.zeros(kv_ref.shape[1:], BF)

    for copy in copies:
        copy.wait()
    project(0, x)
    for t in range(4):
        if t in first:
            arrive(1, x, t)
            x_push(0, 1, x, t, 0)
            x_push(1, 1, x, t, 0)
        arrive(0, left, t)
        if t % 2 == 0:
            x_push(0, 0, left, t, 1)
        if t in late:
            z_push(1, left, t)
        arrive(0, right, t)
        if t % 2 == 1:
            x_push(1, 0, right, t, 1)
        if t in late:
            z_push(2, right, t)
    project(0, left)
    for t in first:
        arrive(1, left, t)
        if t % 2 == 1:
            x_push(0, 1, left, t, 1)
        arrive(1, right, t)
        if t % 2 == 0:
            x_push(1, 1, right, t, 1)
    for t in late:
        arrive(0, opp, t)
        z_push(3, opp, t)
    project(0, right)
    for t in first:
        arrive(0, opp, t)
    project(0, opp)
    w_first.wait_recv()
    w_second = remote(
        wpair_ref.at[mine], wpair_ref.at[mine], wo_sem.at[2], wo_sem.at[3], (me, mate)
    )
    for t in late:
        arrive(1, x, t)
    project(1, x)
    for t in late:
        arrive(1, left, t)
    project(1, left)
    for t in late:
        arrive(1, right, t)
    project(1, right)
    for t in range(4):
        arrive(1, opp, t)
    project(1, opp)

    for copy in sends:
        copy.wait_send()
    w_first.wait_send()
    w_second.wait()

    @pl.when(row < 15)
    def _():
        for copy in kv_up:
            copy.wait_send()
        for copy in kv_down:
            copy.wait_recv()

    @pl.when(row > 0)
    def _():
        for copy in kv_down:
            copy.wait_send()
        for copy in kv_up:
            copy.wait_recv()


def attention_kernel(rw_ref, q_ref, kv_ref, out_ref, bias):
    keys = 3 * 8 * 64
    first = lax.axis_index("row") * 8
    place_of = lax.broadcasted_iota(jnp.int32, (1, keys), 1)
    key_row = (place_of // 512) * 8 + (place_of % 64) // 8
    key_ids = jnp.full((1, keys), -1, jnp.int32)
    for r in range(24):
        row = first + r - 8
        inside = jnp.logical_and(row >= 0, row < 128)
        number = jnp.where(inside, rw_ref[jnp.clip(row, 0, 127)], -1)
        key_ids = jnp.where(key_row == r, number, key_ids)
    for r in range(8):
        line = jnp.where(key_ids == rw_ref[first + r], 0.0, -1e30)
        line = jnp.broadcast_to(line, (8, keys))
        bias[pl.ds(8 * r, 8), :] = line
        bias[pl.ds(64 + 8 * r, 8), :] = line
    factor = HEAD ** (-0.5) * 1.4426950408889634
    for c in range(2):
        for h in range(3):
            key = kv_ref[:, :, c * 64 : c * 64 + 64, h * HEAD : (h + 1) * HEAD].reshape(keys, HEAD)
            value = kv_ref[
                :, :, c * 64 : c * 64 + 64, WIDTH + h * HEAD : WIDTH + (h + 1) * HEAD
            ].reshape(keys, HEAD)

            def block(i, carry):
                at = pl.ds(i * 2, 2)
                query = q_ref[at, c * 64 : c * 64 + 64, h * HEAD : (h + 1) * HEAD].reshape(
                    128, HEAD
                )
                scores = lax.dot_general(
                    query, key, (((1,), (1,)), ((), ())), preferred_element_type=F32
                )
                scores = scores + bias[...]
                highest = jnp.max(scores, axis=1, keepdims=True)
                raised = jnp.exp2((scores - highest) * factor)
                total = jnp.sum(raised, axis=1, keepdims=True)
                result = jnp.dot(raised.astype(BF), value, preferred_element_type=F32)
                result = (result * (1.0 / total)).astype(BF)
                out_ref[at, c * 64 : c * 64 + 64, h * HEAD : (h + 1) * HEAD] = result.reshape(
                    2, 64, HEAD
                )
                return carry

            lax.fori_loop(0, 4, block, 0)


def scatter_kernel(
    shift_ref, att_ref, mixed_ref, wown_ref, wpair_ref, out_ref,
    pair, w, part, inbox, z_sem, send, recv, w_sem,
):
    z, x, row = place()
    me = z * 4 + x
    other = (1 - z) * 4
    right, left, opp = lax.rem(x + 1, 4), lax.rem(x + 3, 4), lax.rem(x + 2, 4)
    loads = []
    for k, source in enumerate((wown_ref, wpair_ref)):
        copy = pltpu.make_async_copy(source, w.at[pl.ds(k * WIDTH, WIDTH)], w_sem.at[k])
        copy.start()
        loads.append(copy)

    barrier = pltpu.get_barrier_semaphore()
    for target in (other + x, z * 4 + right, z * 4 + left):
        pl.semaphore_signal(barrier, inc=1, device_id=(target, row), device_id_type=MESH)
    pl.semaphore_wait(barrier, 3)

    def remote(src, dst, s, r, target):
        copy = pltpu.make_async_remote_copy(
            src_ref=src, dst_ref=dst, send_sem=s, recv_sem=r,
            device_id=(target, row), device_id_type=MESH,
        )
        copy.start()
        return copy

    order = (opp, right, left, x)
    crossing = [
        remote(att_ref.at[other + c], pair.at[k], z_sem.at[0, k], z_sem.at[1, k], other + x)
        for k, c in enumerate(order)
    ]
    for copy in loads:
        copy.wait()

    def compute(k):
        crossing[k].wait_recv()
        tokens = jnp.concatenate([att_ref[z * 4 + order[k]], pair[k]], axis=1)
        for c in range(4):
            lanes = slice(c * CHUNK, (c + 1) * CHUNK)
            part[k, :, :, lanes] = (
                jnp.dot(tokens, w[:, lanes], preferred_element_type=F32)
                .astype(BF)
                .reshape(2, 64, CHUNK)
            )

    def push(direction, slot, k, h):
        to = z * 4 + (right if direction == 0 else left)
        return remote(
            part.at[k, h], inbox.at[direction, slot], send.at[direction, slot],
            recv.at[direction, slot], to,
        )

    compute(0)
    rights = [push(0, 0, 0, 0)]
    lefts = [push(1, 0, 0, 1)]
    compute(1)
    rights.append(push(0, 1, 1, 1))
    compute(2)
    lefts.append(push(1, 1, 2, 0))
    rights[0].wait_recv()
    part[1, 0] = (part[1, 0].astype(F32) + inbox[0, 0].astype(F32)).astype(BF)
    rights.append(push(0, 2, 1, 0))
    lefts[0].wait_recv()
    part[2, 1] = (part[2, 1].astype(F32) + inbox[1, 0].astype(F32)).astype(BF)
    lefts.append(push(1, 2, 2, 1))
    compute(3)

    shift = shift_ref[0]
    rows_p, cols_p = packed_columns(shift, (TOK, TOK), 1)
    target_token = lax.broadcasted_iota(jnp.int32, (TOK, TOK), 0)
    unpick = (target_token == rows_p * 16 + cols_p).astype(F32).astype(BF)
    rights[1].wait_recv()
    lefts[1].wait_recv()
    rights[2].wait_recv()
    lefts[2].wait_recv()
    for c in range(4):
        lanes = slice(c * CHUNK, (c + 1) * CHUNK)
        a, bb = (
            part[3, 0, :, lanes].astype(F32)
            + inbox[0, 2, :, lanes].astype(F32)
            + inbox[1, 1, :, lanes].astype(F32),
            part[3, 1, :, lanes].astype(F32)
            + inbox[0, 1, :, lanes].astype(F32)
            + inbox[1, 2, :, lanes].astype(F32),
        )
        total = jnp.concatenate([a, bb], axis=0) + mixed_ref[:, lanes].astype(F32)
        out_ref[:, lanes] = jnp.dot(
            unpick, total.astype(BF), preferred_element_type=F32
        ).astype(BF)
    for copy in crossing + rights + lefts:
        copy.wait_send()


VM = pl.BlockSpec(memory_space=pltpu.VMEM)
SM = pl.BlockSpec(memory_space=pltpu.SMEM)
ANY = pl.BlockSpec(memory_space=pl.ANY)
DMA = pltpu.SemaphoreType.DMA


def local(base_latent, degraded, row_window, column_shift, norm_gain, project_in, project_out):
    base = base_latent.reshape(8, 4, 4, CHUNK).transpose(0, 2, 1, 3).reshape(8, 16, CHUNK)
    fine = degraded.reshape(TOK, D)
    weights = project_in.transpose(1, 0, 2)
    mixed, query, keyval, wpair = pl.pallas_call(
        gather_kernel,
        out_shape=(
            jax.ShapeDtypeStruct((TOK, D), BF),
            jax.ShapeDtypeStruct((8, TOK, WIDTH), BF),
            jax.ShapeDtypeStruct((3, 8, TOK, 2 * WIDTH), BF),
            jax.ShapeDtypeStruct((WIDTH, D), BF),
        ),
        in_specs=[VM, VM, SM, VM, ANY, ANY],
        out_specs=(VM, VM, VM, ANY),
        scratch_shapes=[
            pltpu.VMEM((8, 4, QTR, D), BF),
            pltpu.VMEM((8, 16, CHUNK), BF),
            pltpu.VMEM((3, D, WIDTH), BF),
            DMA((2, 8)),
            DMA((2, 2, 2, 4)),
            DMA((4, 4)),
            DMA((8, 4)),
            DMA((2, 8)),
            DMA((2, 8)),
            DMA((3,)),
            DMA((4,)),
        ],
        compiler_params=pltpu.CompilerParams(
            collective_id=0, has_side_effects=True, vmem_limit_bytes=56 * 2**20
        ),
        name="gather_project",
    )(base, fine, column_shift, norm_gain.reshape(1, D), weights, project_out)
    attended = pl.pallas_call(
        attention_kernel,
        out_shape=jax.ShapeDtypeStruct((8, TOK, WIDTH), BF),
        in_specs=[SM, VM, VM],
        out_specs=VM,
        scratch_shapes=[pltpu.VMEM((128, 1536), F32)],
        compiler_params=pltpu.CompilerParams(vmem_limit_bytes=48 * 2**20),
        name="attend",
    )(row_window, query, keyval)
    out = pl.pallas_call(
        scatter_kernel,
        out_shape=jax.ShapeDtypeStruct((TOK, D), BF),
        in_specs=[SM, VM, VM, ANY, ANY],
        out_specs=VM,
        scratch_shapes=[
            pltpu.VMEM((4, TOK, WIDTH), BF),
            pltpu.VMEM((2 * WIDTH, D), BF),
            pltpu.VMEM((4, 2, 64, D), BF),
            pltpu.VMEM((2, 3, 64, D), BF),
            DMA((2, 4)),
            DMA((2, 3)),
            DMA((2, 3)),
            DMA((2,)),
        ],
        compiler_params=pltpu.CompilerParams(
            collective_id=1, has_side_effects=True, vmem_limit_bytes=56 * 2**20
        ),
        name="project_scatter",
    )(column_shift, attended, mixed, project_out, wpair)
    return out.reshape(1, 8, 16, D)


def solution(mesh):
    placed = (
        P(None, "row", "frame", None),
        P("frame", "row", None, None),
        P(),
        P(),
        P(),
        P(None, None, "frame"),
        P("frame", None),
    )
    return jax.shard_map(
        local, mesh=mesh, in_specs=placed, out_specs=P("frame", "row", None, None), check_vma=False
    )
```

```python
import jax
import jax.numpy as jnp
from jax import lax
from jax.experimental import pallas as pl
from jax.experimental.pallas import tpu as pltpu
from jax.sharding import PartitionSpec as P

MESH = pl.DeviceIdType.MESH
HEAD = 128
D = 3072
TOK = 128
SIDE = 64
QTR = 32
WIDTH = 384
CHUNK = 768
BF = jnp.bfloat16
F32 = jnp.float32
FACTOR = HEAD ** (-0.5) * 1.4426950408889634


def packed_place(shift, token):
    column = (token // SIDE) * 8 + token % 8 + shift
    column = jnp.where(column >= 16, column - 16, column)
    return (token // 8) % 8, column


def one_hot(mask):
    return jnp.where(mask, 1.0, 0.0).astype(BF)


def layer_kernel(
    base_ref, deg_ref, shift_ref, rw_ref, gain_ref, win_ref, wout_ref,
    out_ref,
    g, b, w, wo, mixed, q, kv, att, pair, part, inbox, bias_own, bias_rim,
    base_sem, x_send, z_send, g_recv, kv_send, kv_recv, w_sem, wo_sem,
    pair_send, pair_recv, part_send, part_recv,
):
    row = lax.axis_index("row")
    me = lax.axis_index("frame")
    z, x = me // 4, me % 4
    here, other = z * 4, (1 - z) * 4
    right, left, opp = lax.rem(x + 1, 4), lax.rem(x + 3, 4), lax.rem(x + 2, 4)
    mate = row + 1 - 2 * lax.rem(row, 2)
    outer = row + 2 * lax.rem(row, 2) - 1
    far_row = lax.rem(row + 8, 16)

    loads = []
    for k in range(3):
        copy = pltpu.make_async_copy(win_ref.at[k], w.at[k], w_sem.at[k])
        copy.start()
        loads.append(copy)
    own_out = pltpu.make_async_copy(wout_ref, wo.at[pl.ds(0, WIDTH)], w_sem.at[3])
    own_out.start()

    barrier = pltpu.get_barrier_semaphore()
    for step in range(1, 8):
        pl.semaphore_signal(
            barrier, inc=1, device_id=(lax.rem(me + step, 8), row), device_id_type=MESH
        )
    for target in ((me, mate), (other + x, far_row)):
        pl.semaphore_signal(barrier, inc=1, device_id=target, device_id_type=MESH)
    has_outer = jnp.logical_and(outer >= 0, outer < 16)

    @pl.when(has_outer)
    def _():
        pl.semaphore_signal(barrier, inc=1, device_id=(me, outer), device_id_type=MESH)

    shift = shift_ref[0]
    token = lax.broadcasted_iota(jnp.int32, (TOK, TOK), 0)
    source = lax.broadcasted_iota(jnp.int32, (TOK, TOK), 1)
    rows_q, cols_q = packed_place(shift, token)
    pick_fine = one_hot(source == rows_q * 16 + cols_q)
    for c in range(4):
        lanes = slice(c * CHUNK, (c + 1) * CHUNK)
        mixed[:, lanes] = jnp.dot(
            pick_fine, deg_ref[:, lanes], preferred_element_type=F32
        ).astype(BF)

    @pl.when(has_outer)
    def _():
        pl.semaphore_wait(barrier, 10)

    @pl.when(jnp.logical_not(has_outer))
    def _():
        pl.semaphore_wait(barrier, 9)

    def remote(src, dst, send, recv, target):
        copy = pltpu.make_async_remote_copy(
            src_ref=src, dst_ref=dst, send_sem=send, recv_sem=recv,
            device_id=target, device_id_type=MESH,
        )
        copy.start()
        return copy

    base_copies = []
    for step in range(1, 8):
        to = lax.rem(me + step, 8)
        base_copies.append(
            remote(base_ref.at[to], b.at[me], base_sem.at[0, step], base_sem.at[1, step], (to, row))
        )
    own_base = pltpu.make_async_copy(base_ref.at[me], b.at[me], base_sem.at[0, 0])
    own_base.start()

    sends = []

    def item(plane, column):
        return (here if plane == 0 else other) + column

    def x_push(direction, plane, column, t, forward=0):
        frame = item(plane, column)
        to = right if direction == 0 else left
        sends.append(
            remote(g.at[frame, t], g.at[frame, t], x_send.at[direction, plane, forward, t],
                   g_recv.at[frame, t], (here + to, row))
        )

    def z_push(slot, column, t):
        frame = item(0, column)
        sends.append(
            remote(g.at[frame, t], g.at[frame, t], z_send.at[slot, t],
                   g_recv.at[frame, t], (other + x, row))
        )

    def arrive(plane, column, t):
        frame = item(plane, column)
        pltpu.make_async_remote_copy(
            src_ref=g.at[frame, t], dst_ref=g.at[frame, t], send_sem=z_send.at[0, 0],
            recv_sem=g_recv.at[frame, t], device_id=(other + x, row), device_id_type=MESH,
        ).wait_recv()

    def heading(plane, t):
        return (t // 2 + plane) % 2

    own_base.wait()
    for copy in base_copies:
        copy.wait()
    coarse = jnp.concatenate([b[j] for j in range(8)], axis=0)

    def mix(c):
        rows = slice(c * SIDE, (c + 1) * SIDE)
        fine = lax.broadcasted_iota(jnp.int32, (SIDE, QTR), 0) + c * SIDE
        at = lax.broadcasted_iota(jnp.int32, (SIDE, QTR), 1)
        rows_c, cols_c = packed_place(shift, fine)
        pick = one_hot(at == (cols_c // 2) * 4 + rows_c // 2)
        square = jnp.zeros((SIDE, 1), F32)
        for k in range(4):
            lanes = slice(k * CHUNK, (k + 1) * CHUNK)
            up = jnp.dot(pick, coarse[:, lanes], preferred_element_type=F32)
            total = (up + mixed[rows, lanes].astype(F32)).astype(BF)
            mixed[rows, lanes] = total
            total = total.astype(F32)
            square = square + jnp.sum(total * total, axis=1, keepdims=True)
        scale = lax.rsqrt(square * (1.0 / D) + 1e-06)
        for k in range(4):
            lanes = slice(k * CHUNK, (k + 1) * CHUNK)
            normed = mixed[rows, lanes].astype(F32) * scale * gain_ref[:, lanes]
            g[me, 2 * c : 2 * c + 2, :, lanes] = normed.astype(BF).reshape(2, QTR, CHUNK)

    def push_own(c):
        a, l = 2 * c, 2 * c + 1
        z_push(0, x, a)
        x_push(0, 0, x, a)
        x_push(1, 0, x, a)
        x_push(0, 0, x, l)
        x_push(1, 0, x, l)
        z_push(0, x, l)

    def wave_one(c):
        a, l = 2 * c, 2 * c + 1
        arrive(1, x, a)
        x_push(0, 1, x, a)
        x_push(1, 1, x, a)
        for t in (a, l):
            arrive(0, left, t)
            if heading(0, t) == 0:
                x_push(0, 0, left, t, 1)
            if t == l:
                z_push(1, left, t)
            arrive(0, right, t)
            if heading(0, t) == 1:
                x_push(1, 0, right, t, 1)
            if t == l:
                z_push(2, right, t)

    def wave_two(c):
        a, l = 2 * c, 2 * c + 1
        arrive(1, left, a)
        if heading(1, a) == 0:
            x_push(0, 1, left, a, 1)
        arrive(1, right, a)
        if heading(1, a) == 1:
            x_push(1, 1, right, a, 1)
        arrive(0, opp, l)
        z_push(3, opp, l)
        arrive(0, opp, a)

    kv_copies = ([], [])

    def project(c, *pieces):
        frames = [item(plane, column) for plane, column in pieces]
        tokens = jnp.concatenate(
            [g[frame, 2 * c : 2 * c + 2].reshape(SIDE, D) for frame in frames], axis=0
        )
        for k in range(3):
            result = jnp.dot(tokens, w[k], preferred_element_type=F32)
            if k == 0:
                result = result * FACTOR
            result = result.astype(BF)
            for i, frame in enumerate(frames):
                value = result[i * SIDE : (i + 1) * SIDE]
                if k == 0:
                    q[c, frame] = value
                else:
                    kv[1, c, frame, :, (k - 1) * WIDTH : k * WIDTH] = value
        for frame in frames:
            n = len(kv_copies[c])
            up = pltpu.make_async_remote_copy(
                src_ref=kv.at[1, c, frame], dst_ref=kv.at[0, c, frame],
                send_sem=kv_send.at[0, c, n], recv_sem=kv_recv.at[0, c, n],
                device_id=(me, row + 1), device_id_type=MESH,
            )
            down = pltpu.make_async_remote_copy(
                src_ref=kv.at[1, c, frame], dst_ref=kv.at[2, c, frame],
                send_sem=kv_send.at[1, c, n], recv_sem=kv_recv.at[1, c, n],
                device_id=(me, row - 1), device_id_type=MESH,
            )
            kv_copies[c].append((up, down))

            @pl.when(row < 15)
            def _():
                up.start()

            @pl.when(row > 0)
            def _():
                down.start()

    def attend(c):
        @pl.when(row > 0)
        def _():
            for up, down in kv_copies[c]:
                up.wait_recv()

        @pl.when(row < 15)
        def _():
            for up, down in kv_copies[c]:
                down.wait_recv()

        even = (lax.broadcasted_iota(jnp.int32, (SIDE, 2 * WIDTH), 0) // 8) % 2 == 0

        def merge(f, carry):
            kv[3, c, f] = jnp.where(
                even, kv[2, c, f].astype(F32), kv[0, c, f].astype(F32)
            ).astype(BF)
            return carry

        lax.fori_loop(0, 8, merge, 0)
        two = lax.broadcasted_iota(jnp.int32, (TOK, HEAD), 0)
        lane = lax.broadcasted_iota(jnp.int32, (TOK, HEAD), 1)
        query_row = one_hot((two // 8) % 2 == lane)
        ones = jnp.ones((2 * 512, HEAD), BF)

        def block(j, carry):
            at = pl.ds(pl.multiple_of(j * 16, 16), 16)
            own_bias = bias_own[j].reshape(512, HEAD)
            rim_bias = bias_rim[j]
            bias = jnp.concatenate([own_bias, rim_bias], axis=0)
            for h in range(3):
                kl = slice(h * HEAD, (h + 1) * HEAD)
                vl = slice(WIDTH + h * HEAD, WIDTH + (h + 1) * HEAD)
                query = q[c, :, at, kl].reshape(TOK, HEAD)
                keys = [kv[1, c, :, :, kl].reshape(512, HEAD)]
                values = [kv[1, c, :, :, vl].reshape(512, HEAD)]
                for p in range(4):
                    band = jnp.where(j > p, 2, jnp.where(j == p, 3, 0))
                    keys.append(kv[band, c, :, 16 * p : 16 * p + 16, kl].reshape(TOK, HEAD))
                    values.append(kv[band, c, :, 16 * p : 16 * p + 16, vl].reshape(TOK, HEAD))
                key = jnp.concatenate([jnp.concatenate(keys, axis=0), bias], axis=1)
                value = jnp.concatenate([jnp.concatenate(values, axis=0), ones], axis=1)
                scores = lax.dot_general(
                    jnp.concatenate([query, query_row], axis=1), key,
                    (((1,), (1,)), ((), ())), preferred_element_type=F32,
                )
                raised = jnp.exp2(scores - jnp.max(scores, axis=1, keepdims=True))
                result = jnp.dot(raised.astype(BF), value, preferred_element_type=F32)
                result = result[:, :HEAD] / result[:, HEAD:]
                att[c, :, at, kl] = result.astype(BF).reshape(8, 16, HEAD)
            return carry

        lax.fori_loop(0, 4, block, 0)

    order = (opp, right, left, x)
    crossing = ([], [])

    def cross(c):
        for k, column in enumerate(order):
            crossing[c].append(
                remote(att.at[c, other + column], pair.at[c, k], pair_send.at[c, k],
                       pair_recv.at[c, k], (other + x, row))
            )

    def multiply(c, first):
        halves = []
        for k in (first, first + 1):
            crossing[c][k].wait_recv()
            halves.append(jnp.concatenate([att[c, here + order[k]], pair[c, k]], axis=1))
        tokens = jnp.concatenate(halves, axis=0)
        for n in range(4):
            lanes = slice(n * CHUNK, (n + 1) * CHUNK)
            part[c, first : first + 2, :, :, lanes] = (
                jnp.dot(tokens, wo[:, lanes], preferred_element_type=F32)
                .astype(BF)
                .reshape(2, 2, QTR, CHUNK)
            )

    ring = {}

    def push(c, direction, slot, k, h):
        to = right if direction == 0 else left
        ring[c, direction, slot] = remote(
            part.at[c, k, h], inbox.at[c, direction, slot], part_send.at[c, direction, slot],
            part_recv.at[c, direction, slot], (here + to, row),
        )

    def scatter_start(c):
        multiply(c, 0)
        push(c, 0, 0, 0, 0)
        push(c, 1, 0, 0, 1)
        push(c, 0, 1, 1, 1)
        multiply(c, 2)
        push(c, 1, 1, 2, 0)

    def scatter_next(c):
        ring[c, 0, 0].wait_recv()
        part[c, 1, 0] = (part[c, 1, 0].astype(F32) + inbox[c, 0, 0].astype(F32)).astype(BF)
        push(c, 0, 2, 1, 0)
        ring[c, 1, 0].wait_recv()
        part[c, 2, 1] = (part[c, 2, 1].astype(F32) + inbox[c, 1, 0].astype(F32)).astype(BF)
        push(c, 1, 2, 2, 1)

    def scatter_end(c):
        for direction in range(2):
            for slot in (1, 2):
                ring[c, direction, slot].wait_recv()
        for h in range(2):
            rows = slice(c * SIDE + h * QTR, c * SIDE + (h + 1) * QTR)
            total = part[c, 3, h].astype(F32) + inbox[c, 0, 2 - h].astype(F32)
            total = total + inbox[c, 1, 1 + h].astype(F32)
            mixed[rows, :] = (total + mixed[rows, :].astype(F32)).astype(BF)

    mix(0)
    push_own(0)
    mix(1)

    first_row = row * 8
    lane = lax.broadcasted_iota(jnp.int32, (16, HEAD), 1)
    second = lax.broadcasted_iota(jnp.int32, (16, HEAD), 0) // 8

    def number_of(at):
        inside = jnp.logical_and(at >= 0, at < 128)
        return jnp.where(inside, rw_ref[jnp.clip(at, 0, 127)], -1)

    for j in range(4):
        for p in range(4):
            for rim in range(2):
                tile = jnp.zeros((16, HEAD), F32)
                for s in range(2):
                    i = 2 * p + s
                    key_row = first_row + i
                    if rim:
                        key_row = key_row + (8 if i <= 2 * j else -8)
                    key_number = number_of(key_row)
                    for l in range(2):
                        off = key_number != rw_ref[first_row + 2 * j + l]
                        level = jnp.where(off, -1e30, 0.0)
                        tile = jnp.where(
                            jnp.logical_and(lane == l, second == s), level, tile
                        )
                tile = jnp.broadcast_to(tile.astype(BF)[None], (8, 16, HEAD))
                if rim:
                    bias_rim[j, p * TOK : (p + 1) * TOK, :] = tile.reshape(TOK, HEAD)
                else:
                    bias_own[j, :, 16 * p : 16 * p + 16, :] = tile

    own_out.wait()
    half = WIDTH // 2
    core = lax.rem(row, 2)
    mine = wo.at[pl.ds(pl.multiple_of(core * half, half), half)]
    theirs = wo.at[pl.ds(pl.multiple_of(WIDTH + core * half, half), half)]
    wo_first = remote(mine, theirs, wo_sem.at[0], wo_sem.at[1], (other + x, far_row))

    @pl.when(row == 0)
    def _():
        kv[0] = jnp.zeros((2, 8, SIDE, 2 * WIDTH), BF)

    @pl.when(row == 15)
    def _():
        kv[2] = jnp.zeros((2, 8, SIDE, 2 * WIDTH), BF)

    wave_one(0)
    push_own(1)
    for copy in loads:
        copy.wait()
    project(0, (0, x), (0, left))
    wave_two(0)
    project(0, (0, right), (0, opp))
    arrive(1, x, 1)
    arrive(1, left, 1)
    project(0, (1, x), (1, left))
    wave_one(1)
    arrive(1, right, 1)
    arrive(1, opp, 0)
    arrive(1, opp, 1)
    project(0, (1, right), (1, opp))
    wo_first.wait_recv()
    wo_second = remote(theirs, theirs, wo_sem.at[2], wo_sem.at[3], (me, mate))
    project(1, (0, x), (0, left))
    wave_two(1)
    attend(0)
    cross(0)
    project(1, (0, right), (0, opp))
    arrive(1, x, 3)
    arrive(1, left, 3)
    project(1, (1, x), (1, left))
    arrive(1, right, 3)
    arrive(1, opp, 2)
    arrive(1, opp, 3)
    project(1, (1, right), (1, opp))
    wo_second.wait_recv()
    scatter_start(0)
    attend(1)
    cross(1)
    scatter_next(0)
    scatter_start(1)
    scatter_end(0)
    scatter_next(1)
    scatter_end(1)

    rows_p, cols_p = packed_place(shift, source)
    unpick = one_hot(token == rows_p * 16 + cols_p)
    for c in range(4):
        lanes = slice(c * CHUNK, (c + 1) * CHUNK)
        out_ref[:, lanes] = jnp.dot(
            unpick, mixed[:, lanes], preferred_element_type=F32
        ).astype(BF)

    for copy in sends:
        copy.wait_send()
    wo_first.wait_send()
    wo_second.wait_send()
    for c in range(2):
        for copy in crossing[c]:
            copy.wait_send()
        for direction in range(2):
            for slot in range(3):
                ring[c, direction, slot].wait_send()

    @pl.when(row < 15)
    def _():
        for c in range(2):
            for up, down in kv_copies[c]:
                up.wait_send()

    @pl.when(row > 0)
    def _():
        for c in range(2):
            for up, down in kv_copies[c]:
                down.wait_send()


VM = pl.BlockSpec(memory_space=pltpu.VMEM)
SM = pl.BlockSpec(memory_space=pltpu.SMEM)
ANY = pl.BlockSpec(memory_space=pl.ANY)
DMA = pltpu.SemaphoreType.DMA


def local(base_latent, degraded, row_window, column_shift, norm_gain, project_in, project_out):
    out = pl.pallas_call(
        layer_kernel,
        out_shape=jax.ShapeDtypeStruct((TOK, D), BF),
        in_specs=[VM, VM, SM, SM, VM, ANY, ANY],
        out_specs=VM,
        scratch_shapes=[
            pltpu.VMEM((8, 4, QTR, D), BF),
            pltpu.VMEM((8, 4, D), BF),
            pltpu.VMEM((3, D, WIDTH), BF),
            pltpu.VMEM((2 * WIDTH, D), BF),
            pltpu.VMEM((TOK, D), BF),
            pltpu.VMEM((2, 8, SIDE, WIDTH), BF),
            pltpu.VMEM((4, 2, 8, SIDE, 2 * WIDTH), BF),
            pltpu.VMEM((2, 8, SIDE, WIDTH), BF),
            pltpu.VMEM((2, 4, SIDE, WIDTH), BF),
            pltpu.VMEM((2, 4, 2, QTR, D), BF),
            pltpu.VMEM((2, 2, 3, QTR, D), BF),
            pltpu.VMEM((4, 8, SIDE, HEAD), BF),
            pltpu.VMEM((4, 4 * TOK, HEAD), BF),
            DMA((2, 8)),
            DMA((2, 2, 2, 4)),
            DMA((4, 4)),
            DMA((8, 4)),
            DMA((2, 2, 8)),
            DMA((2, 2, 8)),
            DMA((4,)),
            DMA((4,)),
            DMA((2, 4)),
            DMA((2, 4)),
            DMA((2, 2, 3)),
            DMA((2, 2, 3)),
        ],
        compiler_params=pltpu.CompilerParams(
            collective_id=0, has_side_effects=True, vmem_limit_bytes=60 * 2**20
        ),
        name="layer",
    )(
        base_latent.reshape(8, 4, D),
        degraded.reshape(TOK, D),
        column_shift,
        row_window,
        norm_gain.reshape(1, D),
        project_in.transpose(1, 0, 2),
        project_out,
    )
    return out.reshape(1, 8, 16, D)


def solution(mesh):
    placed = (
        P(None, "row", "frame", None),
        P("frame", "row", None, None),
        P(),
        P(),
        P(),
        P(None, None, "frame"),
        P("frame", None),
    )
    return jax.shard_map(
        local, mesh=mesh, in_specs=placed, out_specs=P("frame", "row", None, None), check_vma=False
    )
```

```python
import jax
import jax.numpy as jnp
from jax import lax
from jax.experimental import pallas as pl
from jax.experimental.pallas import tpu as pltpu
from jax.sharding import PartitionSpec as P

MESH = pl.DeviceIdType.MESH
HEAD = 128
D = 3072
TOK = 128
SIDE = 64
QTR = 32
WIDTH = 384
CHUNK = 768
BF = jnp.bfloat16
F32 = jnp.float32
PIECE = 16
FIRST = ((0, 1, 2), (4, 5, 6))
LATE = ((3,), (7,))
HEADING = {}
for PIECES in zip(FIRST, LATE):
    for GROUP, PLANE in ((0, 1), (0, 0), (1, 0)):
        for T in PIECES[GROUP]:
            HEADING[PLANE, T] = len(HEADING) % 2
FACTOR = HEAD ** (-0.5) * 1.4426950408889634


def packed_place(shift, token):
    column = (token // SIDE) * 8 + token % 8 + shift
    column = jnp.where(column >= 16, column - 16, column)
    return (token // 8) % 8, column


def one_hot(mask):
    return jnp.where(mask, 1.0, 0.0).astype(BF)


def layer_kernel(
    base_ref, deg_ref, shift_ref, rw_ref, gain_ref, win_ref, wout_ref,
    out_ref,
    deg, g, b, w, wo, mixed, q, kv, att, pair, part, inbox, bias,
    base_sem, x_send, z_send, g_recv, kv_send, kv_recv, w_sem, wo_sem,
    pair_send, pair_recv, part_send, part_recv,
):
    row = lax.axis_index("row")
    me = lax.axis_index("frame")
    z, x = me // 4, me % 4
    here, other = z * 4, (1 - z) * 4
    right, left, opp = lax.rem(x + 1, 4), lax.rem(x + 3, 4), lax.rem(x + 2, 4)
    mate = row + 1 - 2 * lax.rem(row, 2)
    outer = row + 2 * lax.rem(row, 2) - 1
    far_row = lax.rem(row + 8, 16)

    barrier = pltpu.get_barrier_semaphore()
    for step in range(1, 8):
        pl.semaphore_signal(
            barrier, inc=1, device_id=(lax.rem(me + step, 8), row), device_id_type=MESH
        )
    for target in ((me, mate), (other + x, far_row)):
        pl.semaphore_signal(barrier, inc=1, device_id=target, device_id_type=MESH)
    has_outer = jnp.logical_and(outer >= 0, outer < 16)

    @pl.when(has_outer)
    def _():
        pl.semaphore_signal(barrier, inc=1, device_id=(me, outer), device_id_type=MESH)

    deg_load = pltpu.make_async_copy(deg_ref, deg, w_sem.at[4])
    deg_load.start()
    loads = []
    for k in range(3):
        copy = pltpu.make_async_copy(win_ref.at[k], w.at[k], w_sem.at[k])
        copy.start()
        loads.append(copy)
    own_out = pltpu.make_async_copy(wout_ref, wo.at[pl.ds(0, WIDTH)], w_sem.at[3])
    own_out.start()

    shift = shift_ref[0]
    token = lax.broadcasted_iota(jnp.int32, (TOK, TOK), 0)
    source = lax.broadcasted_iota(jnp.int32, (TOK, TOK), 1)
    rows_q, cols_q = packed_place(shift, token)
    pick_fine = one_hot(source == rows_q * 16 + cols_q)
    deg_load.wait()
    for c in range(4):
        lanes = slice(c * CHUNK, (c + 1) * CHUNK)
        mixed[:, lanes] = jnp.dot(
            pick_fine, deg[:, lanes], preferred_element_type=F32
        ).astype(BF)

    @pl.when(has_outer)
    def _():
        pl.semaphore_wait(barrier, 10)

    @pl.when(jnp.logical_not(has_outer))
    def _():
        pl.semaphore_wait(barrier, 9)

    def remote(src, dst, send, recv, target):
        copy = pltpu.make_async_remote_copy(
            src_ref=src, dst_ref=dst, send_sem=send, recv_sem=recv,
            device_id=target, device_id_type=MESH,
        )
        copy.start()
        return copy

    base_copies = []
    for step in range(1, 8):
        to = lax.rem(me + step, 8)
        base_copies.append(
            remote(base_ref.at[to], b.at[me], base_sem.at[0, step], base_sem.at[1, step], (to, row))
        )
    own_base = pltpu.make_async_copy(base_ref.at[me], b.at[me], base_sem.at[0, 0])
    own_base.start()

    sends = []

    def item(plane, column):
        return (here if plane == 0 else other) + column

    def x_push(direction, plane, column, t, forward=0):
        frame = item(plane, column)
        to = right if direction == 0 else left
        sends.append(
            remote(g.at[frame, t], g.at[frame, t], x_send.at[direction, plane, forward, t],
                   g_recv.at[frame, t], (here + to, row))
        )

    def z_push(slot, column, t):
        frame = item(0, column)
        sends.append(
            remote(g.at[frame, t], g.at[frame, t], z_send.at[slot, t],
                   g_recv.at[frame, t], (other + x, row))
        )

    def arrive(plane, column, t):
        frame = item(plane, column)
        pltpu.make_async_remote_copy(
            src_ref=g.at[frame, t], dst_ref=g.at[frame, t], send_sem=z_send.at[0, 0],
            recv_sem=g_recv.at[frame, t], device_id=(other + x, row), device_id_type=MESH,
        ).wait_recv()

    own_base.wait()
    for copy in base_copies:
        copy.wait()
    coarse = jnp.concatenate([b[j] for j in range(8)], axis=0)

    def mix(c):
        rows = slice(c * SIDE, (c + 1) * SIDE)
        fine = lax.broadcasted_iota(jnp.int32, (SIDE, QTR), 0) + c * SIDE
        at = lax.broadcasted_iota(jnp.int32, (SIDE, QTR), 1)
        rows_c, cols_c = packed_place(shift, fine)
        pick = one_hot(at == (cols_c // 2) * 4 + rows_c // 2)
        square = jnp.zeros((SIDE, 1), F32)
        for k in range(4):
            lanes = slice(k * CHUNK, (k + 1) * CHUNK)
            up = jnp.dot(pick, coarse[:, lanes], preferred_element_type=F32)
            total = (up + mixed[rows, lanes].astype(F32)).astype(BF)
            mixed[rows, lanes] = total
            total = total.astype(F32)
            square = square + jnp.sum(total * total, axis=1, keepdims=True)
        scale = lax.rsqrt(square * (1.0 / D) + 1e-06)
        for k in range(4):
            lanes = slice(k * CHUNK, (k + 1) * CHUNK)
            normed = mixed[rows, lanes].astype(F32) * scale * gain_ref[:, lanes]
            g[me, 4 * c : 4 * c + 4, :, lanes] = normed.astype(BF).reshape(4, PIECE, CHUNK)

    def push_own(c):
        for t in FIRST[c]:
            z_push(0, x, t)
        for t in FIRST[c] + LATE[c]:
            x_push(0, 0, x, t)
            x_push(1, 0, x, t)
        for t in LATE[c]:
            z_push(0, x, t)

    def wave_one(c):
        for t in FIRST[c]:
            arrive(1, x, t)
            x_push(0, 1, x, t)
            x_push(1, 1, x, t)
        for t in FIRST[c] + LATE[c]:
            arrive(0, left, t)
            if HEADING[0, t] == 0:
                x_push(0, 0, left, t, 1)
            if t in LATE[c]:
                z_push(1, left, t)
            arrive(0, right, t)
            if HEADING[0, t] == 1:
                x_push(1, 0, right, t, 1)
            if t in LATE[c]:
                z_push(2, right, t)

    def wave_two(c):
        for t in FIRST[c]:
            arrive(1, left, t)
            if HEADING[1, t] == 0:
                x_push(0, 1, left, t, 1)
            arrive(1, right, t)
            if HEADING[1, t] == 1:
                x_push(1, 1, right, t, 1)
        for t in LATE[c]:
            arrive(0, opp, t)
            z_push(3, opp, t)
        for t in FIRST[c]:
            arrive(0, opp, t)

    def wave_three(c):
        for column in (x, left):
            for t in LATE[c]:
                arrive(1, column, t)

    def wave_four(c):
        for t in LATE[c]:
            arrive(1, right, t)
        for t in FIRST[c] + LATE[c]:
            arrive(1, opp, t)

    kv_copies = ([], [])

    def project(c, *pieces):
        frames = [item(plane, column) for plane, column in pieces]
        tokens = jnp.concatenate(
            [g[frame, 4 * c : 4 * c + 4].reshape(SIDE, D) for frame in frames], axis=0
        )
        for k in range(3):
            result = jnp.dot(tokens, w[k], preferred_element_type=F32)
            if k == 0:
                result = result * FACTOR
            result = result.astype(BF)
            for i, frame in enumerate(frames):
                value = result[i * SIDE : (i + 1) * SIDE]
                if k == 0:
                    q[c, frame] = value
                else:
                    kv[1, c, frame, :, (k - 1) * WIDTH : k * WIDTH] = value
        for frame in frames:
            n = len(kv_copies[c])
            up = pltpu.make_async_remote_copy(
                src_ref=kv.at[1, c, frame], dst_ref=kv.at[0, c, frame],
                send_sem=kv_send.at[0, c, n], recv_sem=kv_recv.at[0, c, n],
                device_id=(me, row + 1), device_id_type=MESH,
            )
            down = pltpu.make_async_remote_copy(
                src_ref=kv.at[1, c, frame], dst_ref=kv.at[2, c, frame],
                send_sem=kv_send.at[1, c, n], recv_sem=kv_recv.at[1, c, n],
                device_id=(me, row - 1), device_id_type=MESH,
            )
            kv_copies[c].append((up, down))

            @pl.when(row < 15)
            def _():
                up.start()

            @pl.when(row > 0)
            def _():
                down.start()

    def attend(c):
        @pl.when(row > 0)
        def _():
            for up, down in kv_copies[c]:
                up.wait_recv()

        @pl.when(row < 15)
        def _():
            for up, down in kv_copies[c]:
                down.wait_recv()

        even = (lax.broadcasted_iota(jnp.int32, (SIDE, 2 * WIDTH), 0) // 8) % 2 == 0

        def merge(f, carry):
            kv[3, c, f] = jnp.where(
                even, kv[2, c, f].astype(F32), kv[0, c, f].astype(F32)
            ).astype(BF)
            return carry

        lax.fori_loop(0, 8, merge, 0)
        ones = jnp.ones((2 * 512, HEAD), BF)

        def head(h, carry):
            kl = pl.ds(pl.multiple_of(h * HEAD, HEAD), HEAD)
            vl = pl.ds(pl.multiple_of(WIDTH + h * HEAD, HEAD), HEAD)
            own_key = kv[1, c, :, :, kl].reshape(512, HEAD)
            own_value = kv[1, c, :, :, vl].reshape(512, HEAD)
            for j in range(4):
                at = slice(16 * j, 16 * j + 16)
                keys, values = [own_key], [own_value]
                for p in range(4):
                    band = 2 if j > p else (3 if j == p else 0)
                    rows = slice(16 * p, 16 * p + 16)
                    keys.append(kv[band, c, :, rows, kl].reshape(TOK, HEAD))
                    values.append(kv[band, c, :, rows, vl].reshape(TOK, HEAD))
                value = jnp.concatenate([jnp.concatenate(values, axis=0), ones], axis=1)
                scores = lax.dot_general(
                    q[c, :, at, kl].reshape(TOK, HEAD), jnp.concatenate(keys, axis=0),
                    (((1,), (1,)), ((), ())), preferred_element_type=F32,
                )
                scores = (scores.reshape(8, 16, 2 * 512) + bias[j][None]).reshape(TOK, 2 * 512)
                raised = jnp.exp2(scores - jnp.max(scores, axis=1, keepdims=True))
                result = jnp.dot(raised.astype(BF), value, preferred_element_type=F32)
                result = result[:, :HEAD] / result[:, HEAD:]
                att[c, h, :, at, :] = result.astype(BF).reshape(8, 16, HEAD)
            cross(c, h).start()
            return carry

        lax.fori_loop(0, 3, head, 0)

    def cross(c, h):
        return pltpu.make_async_remote_copy(
            src_ref=att.at[c, h, pl.ds(other, 4)], dst_ref=pair.at[c, h],
            send_sem=pair_send.at[c, h], recv_sem=pair_recv.at[c, h],
            device_id=(other + x, row), device_id_type=MESH,
        )

    order = (opp, right, left, x)

    def multiply(c, first):
        halves = []
        for k in (first, first + 1):
            heads = [att[c, h, here + order[k]] for h in range(3)]
            heads += [pair[c, h, order[k]] for h in range(3)]
            halves.append(jnp.concatenate(heads, axis=1))
        tokens = jnp.concatenate(halves, axis=0)
        for n in range(4):
            lanes = slice(n * CHUNK, (n + 1) * CHUNK)
            part[c, first : first + 2, :, :, lanes] = (
                jnp.dot(tokens, wo[:, lanes], preferred_element_type=F32)
                .astype(BF)
                .reshape(2, 2, QTR, CHUNK)
            )

    ring = {}

    def push(c, direction, slot, k, h):
        to = right if direction == 0 else left
        ring[c, direction, slot] = remote(
            part.at[c, k, h], inbox.at[c, direction, slot], part_send.at[c, direction, slot],
            part_recv.at[c, direction, slot], (here + to, row),
        )

    def scatter_start(c):
        for h in range(3):
            cross(c, h).wait_recv()
        multiply(c, 0)
        push(c, 0, 0, 0, 0)
        push(c, 1, 0, 0, 1)
        push(c, 0, 1, 1, 1)
        multiply(c, 2)
        push(c, 1, 1, 2, 0)

    def scatter_next(c):
        ring[c, 0, 0].wait_recv()
        part[c, 1, 0] = (part[c, 1, 0].astype(F32) + inbox[c, 0, 0].astype(F32)).astype(BF)
        push(c, 0, 2, 1, 0)
        ring[c, 1, 0].wait_recv()
        part[c, 2, 1] = (part[c, 2, 1].astype(F32) + inbox[c, 1, 0].astype(F32)).astype(BF)
        push(c, 1, 2, 2, 1)

    def scatter_end(c):
        for direction in range(2):
            for slot in (1, 2):
                ring[c, direction, slot].wait_recv()
        for h in range(2):
            rows = slice(c * SIDE + h * QTR, c * SIDE + (h + 1) * QTR)
            total = part[c, 3, h].astype(F32) + inbox[c, 0, 2 - h].astype(F32)
            total = total + inbox[c, 1, 1 + h].astype(F32)
            out_ref[rows, :] = (total + mixed[rows, :].astype(F32)).astype(BF)

    mix(0)
    push_own(0)
    mix(1)

    first_row = row * 8
    spot = lax.broadcasted_iota(jnp.int32, (16, 2 * 512), 1)
    second = lax.broadcasted_iota(jnp.int32, (16, 2 * 512), 0) // 8
    key_row = jnp.where(
        spot < 512, (spot % SIDE) // 8, 8 + 2 * ((spot - 512) // TOK) + (spot // 8) % 2
    )

    def number_of(at):
        inside = jnp.logical_and(at >= 0, at < 128)
        return jnp.where(inside, rw_ref[jnp.clip(at, 0, 127)], -1)

    for j in range(4):
        query_number = jnp.where(
            second == 0, rw_ref[first_row + 2 * j], rw_ref[first_row + 2 * j + 1]
        )
        key_number = jnp.zeros((16, 2 * 512), jnp.int32)
        for i in range(8):
            key_number = jnp.where(key_row == i, rw_ref[first_row + i], key_number)
            rim = number_of(first_row + i + (8 if i <= 2 * j else -8))
            key_number = jnp.where(key_row == 8 + i, rim, key_number)
        bias[j] = jnp.where(key_number == query_number, 0.0, -1e30)

    own_out.wait()
    half = WIDTH // 2
    core = lax.rem(row, 2)
    mine = wo.at[pl.ds(pl.multiple_of(core * half, half), half)]
    theirs = wo.at[pl.ds(pl.multiple_of(WIDTH + core * half, half), half)]
    wo_first = remote(mine, theirs, wo_sem.at[0], wo_sem.at[1], (other + x, far_row))

    @pl.when(row == 0)
    def _():
        kv[0] = jnp.zeros((2, 8, SIDE, 2 * WIDTH), BF)

    @pl.when(row == 15)
    def _():
        kv[2] = jnp.zeros((2, 8, SIDE, 2 * WIDTH), BF)

    wave_one(0)
    push_own(1)
    for copy in loads:
        copy.wait()
    project(0, (0, x), (0, left))
    wave_two(0)
    project(0, (0, right), (0, opp))
    wave_three(0)
    project(0, (1, x), (1, left))
    wave_one(1)
    wave_four(0)
    project(0, (1, right), (1, opp))
    wo_first.wait_recv()
    wo_second = remote(theirs, theirs, wo_sem.at[2], wo_sem.at[3], (me, mate))
    project(1, (0, x), (0, left))
    wave_two(1)
    attend(0)
    project(1, (0, right), (0, opp))
    wave_three(1)
    project(1, (1, x), (1, left))
    wave_four(1)
    project(1, (1, right), (1, opp))
    wo_second.wait_recv()
    scatter_start(0)
    attend(1)
    scatter_next(0)
    scatter_start(1)
    scatter_end(0)
    scatter_next(1)
    scatter_end(1)
    for copy in sends:
        copy.wait_send()
    wo_first.wait_send()
    wo_second.wait_send()
    for c in range(2):
        for h in range(3):
            cross(c, h).wait_send()
        for direction in range(2):
            for slot in range(3):
                ring[c, direction, slot].wait_send()

    @pl.when(row < 15)
    def _():
        for c in range(2):
            for up, down in kv_copies[c]:
                up.wait_send()

    @pl.when(row > 0)
    def _():
        for c in range(2):
            for up, down in kv_copies[c]:
                down.wait_send()


def unpack_kernel(shift_ref, packed_ref, out_ref):
    packed = lax.broadcasted_iota(jnp.int32, (TOK, TOK), 1)
    rows_p, cols_p = packed_place(shift_ref[0], packed)
    pick = one_hot(lax.broadcasted_iota(jnp.int32, (TOK, TOK), 0) == rows_p * 16 + cols_p)
    out_ref[...] = jnp.dot(pick, packed_ref[...], preferred_element_type=F32).astype(BF)


VM = pl.BlockSpec(memory_space=pltpu.VMEM)
SM = pl.BlockSpec(memory_space=pltpu.SMEM)
ANY = pl.BlockSpec(memory_space=pl.ANY)
DMA = pltpu.SemaphoreType.DMA


def local(base_latent, degraded, row_window, column_shift, norm_gain, project_in, project_out):
    out = pl.pallas_call(
        layer_kernel,
        out_shape=jax.ShapeDtypeStruct((TOK, D), BF),
        in_specs=[ANY, ANY, SM, SM, VM, ANY, ANY],
        out_specs=VM,
        scratch_shapes=[
            pltpu.VMEM((TOK, D), BF),
            pltpu.VMEM((8, 8, PIECE, D), BF),
            pltpu.VMEM((8, 4, D), BF),
            pltpu.VMEM((3, D, WIDTH), BF),
            pltpu.VMEM((2 * WIDTH, D), BF),
            pltpu.VMEM((TOK, D), BF),
            pltpu.VMEM((2, 8, SIDE, WIDTH), BF),
            pltpu.VMEM((4, 2, 8, SIDE, 2 * WIDTH), BF),
            pltpu.VMEM((2, 3, 8, SIDE, HEAD), BF),
            pltpu.VMEM((2, 3, 4, SIDE, HEAD), BF),
            pltpu.VMEM((2, 4, 2, QTR, D), BF),
            pltpu.VMEM((2, 2, 3, QTR, D), BF),
            pltpu.VMEM((4, 16, 2 * 512), F32),
            DMA((2, 8)),
            DMA((2, 2, 2, 8)),
            DMA((4, 8)),
            DMA((8, 8)),
            DMA((2, 2, 8)),
            DMA((2, 2, 8)),
            DMA((5,)),
            DMA((4,)),
            DMA((2, 3)),
            DMA((2, 3)),
            DMA((2, 2, 3)),
            DMA((2, 2, 3)),
        ],
        compiler_params=pltpu.CompilerParams(
            collective_id=0, has_side_effects=True, vmem_limit_bytes=60 * 2**20
        ),
        name="layer",
    )(
        base_latent.reshape(8, 4, D),
        degraded.reshape(TOK, D),
        column_shift,
        row_window,
        norm_gain.reshape(1, D),
        project_in.transpose(1, 0, 2),
        project_out,
    )
    out = pl.pallas_call(
        unpack_kernel,
        out_shape=jax.ShapeDtypeStruct((TOK, D), BF),
        in_specs=[SM, VM],
        out_specs=VM,
        name="unpack",
    )(column_shift, out)
    return out.reshape(1, 8, 16, D)


def solution(mesh):
    placed = (
        P(None, "row", "frame", None),
        P("frame", "row", None, None),
        P(),
        P(),
        P(),
        P(None, None, "frame"),
        P("frame", None),
    )
    return jax.shard_map(
        local, mesh=mesh, in_specs=placed, out_specs=P("frame", "row", None, None), check_vma=False
    )
```

```python
import jax
import jax.numpy as jnp
from jax import lax
from jax.experimental import pallas as pl
from jax.experimental.pallas import tpu as pltpu
from jax.sharding import PartitionSpec as P

MESH = pl.DeviceIdType.MESH
HEAD = 128
D = 3072
TOK = 128
SIDE = 64
QTR = 32
WIDTH = 384
CHUNK = 768
BF = jnp.bfloat16
F32 = jnp.float32
PIECE = 16
FIRST = ((0, 1, 2), (4, 5, 6))
LATE = ((3,), (7,))
HEADING = {}
for PIECES in zip(FIRST, LATE):
    for GROUP, PLANE in ((0, 1), (0, 0), (1, 0)):
        for T in PIECES[GROUP]:
            HEADING[PLANE, T] = len(HEADING) % 2
FACTOR = HEAD ** (-0.5) * 1.4426950408889634


def packed_place(shift, token):
    column = (token // SIDE) * 8 + token % 8 + shift
    column = jnp.where(column >= 16, column - 16, column)
    return (token // 8) % 8, column


def one_hot(mask):
    return jnp.where(mask, 1.0, 0.0).astype(BF)


def layer_kernel(
    base_ref, deg_ref, shift_ref, rw_ref, gain_ref, win_ref, wout_ref,
    out_ref,
    deg, g, b, w, wo, mixed, q, kv, att, pair, part, inbox, bias,
    base_sem, x_send, z_send, g_recv, kv_send, kv_recv, w_sem, wo_sem,
    pair_send, pair_recv, part_send, part_recv,
):
    row = lax.axis_index("row")
    me = lax.axis_index("frame")
    z, x = me // 4, me % 4
    here, other = z * 4, (1 - z) * 4
    right, left, opp = lax.rem(x + 1, 4), lax.rem(x + 3, 4), lax.rem(x + 2, 4)
    mate = row + 1 - 2 * lax.rem(row, 2)
    outer = row + 2 * lax.rem(row, 2) - 1
    far_row = lax.rem(row + 8, 16)

    barrier = pltpu.get_barrier_semaphore()
    for step in range(1, 8):
        pl.semaphore_signal(
            barrier, inc=1, device_id=(lax.rem(me + step, 8), row), device_id_type=MESH
        )
    for target in ((me, mate), (other + x, far_row)):
        pl.semaphore_signal(barrier, inc=1, device_id=target, device_id_type=MESH)
    has_outer = jnp.logical_and(outer >= 0, outer < 16)

    @pl.when(has_outer)
    def _():
        pl.semaphore_signal(barrier, inc=1, device_id=(me, outer), device_id_type=MESH)

    deg_load = pltpu.make_async_copy(deg_ref, deg, w_sem.at[4])
    deg_load.start()
    loads = []
    for k in range(3):
        copy = pltpu.make_async_copy(win_ref.at[k], w.at[k], w_sem.at[k])
        copy.start()
        loads.append(copy)
    own_out = pltpu.make_async_copy(wout_ref, wo.at[pl.ds(0, WIDTH)], w_sem.at[3])
    own_out.start()

    shift = shift_ref[0]
    token = lax.broadcasted_iota(jnp.int32, (TOK, TOK), 0)
    source = lax.broadcasted_iota(jnp.int32, (TOK, TOK), 1)
    rows_q, cols_q = packed_place(shift, token)
    pick_fine = one_hot(source == rows_q * 16 + cols_q)
    deg_load.wait()
    for c in range(4):
        lanes = slice(c * CHUNK, (c + 1) * CHUNK)
        mixed[:, lanes] = jnp.dot(
            pick_fine, deg[:, lanes], preferred_element_type=F32
        ).astype(BF)

    @pl.when(has_outer)
    def _():
        pl.semaphore_wait(barrier, 10)

    @pl.when(jnp.logical_not(has_outer))
    def _():
        pl.semaphore_wait(barrier, 9)

    def remote(src, dst, send, recv, target):
        copy = pltpu.make_async_remote_copy(
            src_ref=src, dst_ref=dst, send_sem=send, recv_sem=recv,
            device_id=target, device_id_type=MESH,
        )
        copy.start()
        return copy

    base_copies = []
    for step in range(1, 8):
        to = lax.rem(me + step, 8)
        base_copies.append(
            remote(base_ref.at[to], b.at[me], base_sem.at[0, step], base_sem.at[1, step], (to, row))
        )
    own_base = pltpu.make_async_copy(base_ref.at[me], b.at[me], base_sem.at[0, 0])
    own_base.start()

    sends = []

    def item(plane, column):
        return (here if plane == 0 else other) + column

    def x_push(direction, plane, column, t, forward=0):
        frame = item(plane, column)
        to = right if direction == 0 else left
        sends.append(
            remote(g.at[frame, t], g.at[frame, t], x_send.at[direction, plane, forward, t],
                   g_recv.at[frame, t], (here + to, row))
        )

    def z_push(slot, column, t):
        frame = item(0, column)
        sends.append(
            remote(g.at[frame, t], g.at[frame, t], z_send.at[slot, t],
                   g_recv.at[frame, t], (other + x, row))
        )

    def arrive(plane, column, t):
        frame = item(plane, column)
        pltpu.make_async_remote_copy(
            src_ref=g.at[frame, t], dst_ref=g.at[frame, t], send_sem=z_send.at[0, 0],
            recv_sem=g_recv.at[frame, t], device_id=(other + x, row), device_id_type=MESH,
        ).wait_recv()

    own_base.wait()
    for copy in base_copies:
        copy.wait()
    coarse = jnp.concatenate([b[j] for j in range(8)], axis=0)

    def mix(c):
        rows = slice(c * SIDE, (c + 1) * SIDE)
        fine = lax.broadcasted_iota(jnp.int32, (SIDE, QTR), 0) + c * SIDE
        at = lax.broadcasted_iota(jnp.int32, (SIDE, QTR), 1)
        rows_c, cols_c = packed_place(shift, fine)
        pick = one_hot(at == (cols_c // 2) * 4 + rows_c // 2)
        square = jnp.zeros((SIDE, 1), F32)
        for k in range(4):
            lanes = slice(k * CHUNK, (k + 1) * CHUNK)
            up = jnp.dot(pick, coarse[:, lanes], preferred_element_type=F32)
            total = (up + mixed[rows, lanes].astype(F32)).astype(BF)
            mixed[rows, lanes] = total
            total = total.astype(F32)
            square = square + jnp.sum(total * total, axis=1, keepdims=True)
        scale = lax.rsqrt(square * (1.0 / D) + 1e-06)
        for k in range(4):
            lanes = slice(k * CHUNK, (k + 1) * CHUNK)
            normed = mixed[rows, lanes].astype(F32) * scale * gain_ref[:, lanes]
            g[me, 4 * c : 4 * c + 4, :, lanes] = normed.astype(BF).reshape(4, PIECE, CHUNK)

    def push_own(c):
        for t in FIRST[c]:
            z_push(0, x, t)
        for t in LATE[c] + FIRST[c]:
            x_push(0, 0, x, t)
            x_push(1, 0, x, t)
        for t in LATE[c]:
            z_push(0, x, t)

    def wave_one(c):
        for t in FIRST[c]:
            arrive(1, x, t)
            x_push(0, 1, x, t)
            x_push(1, 1, x, t)
        for t in LATE[c] + FIRST[c]:
            arrive(0, left, t)
            if HEADING[0, t] == 0:
                x_push(0, 0, left, t, 1)
            if t in LATE[c]:
                z_push(1, left, t)
            arrive(0, right, t)
            if HEADING[0, t] == 1:
                x_push(1, 0, right, t, 1)
            if t in LATE[c]:
                z_push(2, right, t)

    def wave_two(c):
        for t in FIRST[c]:
            arrive(1, left, t)
            if HEADING[1, t] == 0:
                x_push(0, 1, left, t, 1)
            arrive(1, right, t)
            if HEADING[1, t] == 1:
                x_push(1, 1, right, t, 1)
        for t in LATE[c]:
            arrive(0, opp, t)
            z_push(3, opp, t)
        for t in FIRST[c]:
            arrive(0, opp, t)

    def wave_three(c):
        for column in (x, left):
            for t in LATE[c]:
                arrive(1, column, t)

    def wave_four(c):
        for t in LATE[c]:
            arrive(1, right, t)
        for t in FIRST[c] + LATE[c]:
            arrive(1, opp, t)

    kv_copies = ([], [])

    def project(c, *pieces):
        frames = [item(plane, column) for plane, column in pieces]
        tokens = jnp.concatenate(
            [g[frame, 4 * c : 4 * c + 4].reshape(SIDE, D) for frame in frames], axis=0
        )
        for k in range(3):
            result = jnp.dot(tokens, w[k], preferred_element_type=F32)
            if k == 0:
                result = result * FACTOR
            result = result.astype(BF)
            for i, frame in enumerate(frames):
                value = result[i * SIDE : (i + 1) * SIDE]
                if k == 0:
                    q[c, frame] = value
                else:
                    kv[1, c, frame, :, (k - 1) * WIDTH : k * WIDTH] = value
        for frame in frames:
            n = len(kv_copies[c])
            up = pltpu.make_async_remote_copy(
                src_ref=kv.at[1, c, frame], dst_ref=kv.at[0, c, frame],
                send_sem=kv_send.at[0, c, n], recv_sem=kv_recv.at[0, c, n],
                device_id=(me, row + 1), device_id_type=MESH,
            )
            down = pltpu.make_async_remote_copy(
                src_ref=kv.at[1, c, frame], dst_ref=kv.at[2, c, frame],
                send_sem=kv_send.at[1, c, n], recv_sem=kv_recv.at[1, c, n],
                device_id=(me, row - 1), device_id_type=MESH,
            )
            kv_copies[c].append((up, down))

            @pl.when(row < 15)
            def _():
                up.start()

            @pl.when(row > 0)
            def _():
                down.start()

    def attend(c):
        @pl.when(row > 0)
        def _():
            for up, down in kv_copies[c]:
                up.wait_recv()

        @pl.when(row < 15)
        def _():
            for up, down in kv_copies[c]:
                down.wait_recv()

        even = (lax.broadcasted_iota(jnp.int32, (SIDE, 2 * WIDTH), 0) // 8) % 2 == 0

        def merge(f, carry):
            kv[3, c, f] = jnp.where(
                even, kv[2, c, f].astype(F32), kv[0, c, f].astype(F32)
            ).astype(BF)
            return carry

        lax.fori_loop(0, 8, merge, 0)
        ones = jnp.ones((2 * 512, HEAD), BF)

        def head(h, carry):
            kl = pl.ds(pl.multiple_of(h * HEAD, HEAD), HEAD)
            vl = pl.ds(pl.multiple_of(WIDTH + h * HEAD, HEAD), HEAD)
            own_key = kv[1, c, :, :, kl].reshape(512, HEAD)
            own_value = kv[1, c, :, :, vl].reshape(512, HEAD)
            for j in range(4):
                at = slice(16 * j, 16 * j + 16)
                keys, values = [own_key], [own_value]
                for p in range(4):
                    band = 2 if j > p else (3 if j == p else 0)
                    rows = slice(16 * p, 16 * p + 16)
                    keys.append(kv[band, c, :, rows, kl].reshape(TOK, HEAD))
                    values.append(kv[band, c, :, rows, vl].reshape(TOK, HEAD))
                value = jnp.concatenate([jnp.concatenate(values, axis=0), ones], axis=1)
                scores = lax.dot_general(
                    q[c, :, at, kl].reshape(TOK, HEAD), jnp.concatenate(keys, axis=0),
                    (((1,), (1,)), ((), ())), preferred_element_type=F32,
                )
                scores = (scores.reshape(8, 16, 2 * 512) + bias[j][None]).reshape(TOK, 2 * 512)
                raised = jnp.exp2(scores - jnp.max(scores, axis=1, keepdims=True))
                result = jnp.dot(raised.astype(BF), value, preferred_element_type=F32)
                result = result[:, :HEAD] / result[:, HEAD:]
                att[c, h, :, at, :] = result.astype(BF).reshape(8, 16, HEAD)
            cross(c, h).start()
            return carry

        lax.fori_loop(0, 3, head, 0)

    def cross(c, h):
        return pltpu.make_async_remote_copy(
            src_ref=att.at[c, h, pl.ds(other, 4)], dst_ref=pair.at[c, h],
            send_sem=pair_send.at[c, h], recv_sem=pair_recv.at[c, h],
            device_id=(other + x, row), device_id_type=MESH,
        )

    order = (opp, right, left, x)

    def multiply(c, first):
        halves = []
        for k in (first, first + 1):
            heads = [att[c, h, here + order[k]] for h in range(3)]
            heads += [pair[c, h, order[k]] for h in range(3)]
            halves.append(jnp.concatenate(heads, axis=1))
        tokens = jnp.concatenate(halves, axis=0)
        for n in range(4):
            lanes = slice(n * CHUNK, (n + 1) * CHUNK)
            part[c, first : first + 2, :, :, lanes] = (
                jnp.dot(tokens, wo[:, lanes], preferred_element_type=F32)
                .astype(BF)
                .reshape(2, 2, QTR, CHUNK)
            )

    ring = {}

    def push(c, direction, slot, k, h):
        to = right if direction == 0 else left
        ring[c, direction, slot] = remote(
            part.at[c, k, h], inbox.at[c, direction, slot], part_send.at[c, direction, slot],
            part_recv.at[c, direction, slot], (here + to, row),
        )

    def scatter_start(c):
        for h in range(3):
            cross(c, h).wait_recv()
        multiply(c, 0)
        push(c, 0, 0, 0, 0)
        push(c, 1, 0, 0, 1)
        push(c, 0, 1, 1, 1)
        multiply(c, 2)
        push(c, 1, 1, 2, 0)

    def scatter_next(c):
        ring[c, 0, 0].wait_recv()
        part[c, 1, 0] = (part[c, 1, 0].astype(F32) + inbox[c, 0, 0].astype(F32)).astype(BF)
        push(c, 0, 2, 1, 0)
        ring[c, 1, 0].wait_recv()
        part[c, 2, 1] = (part[c, 2, 1].astype(F32) + inbox[c, 1, 0].astype(F32)).astype(BF)
        push(c, 1, 2, 2, 1)

    def scatter_end(c):
        for direction in range(2):
            for slot in (1, 2):
                ring[c, direction, slot].wait_recv()
        for h in range(2):
            rows = slice(c * SIDE + h * QTR, c * SIDE + (h + 1) * QTR)
            total = part[c, 3, h].astype(F32) + inbox[c, 0, 2 - h].astype(F32)
            total = total + inbox[c, 1, 1 + h].astype(F32)
            out_ref[rows, :] = (total + mixed[rows, :].astype(F32)).astype(BF)

    mix(0)
    push_own(0)
    mix(1)

    first_row = row * 8
    spot = lax.broadcasted_iota(jnp.int32, (16, 2 * 512), 1)
    second = lax.broadcasted_iota(jnp.int32, (16, 2 * 512), 0) // 8
    key_row = jnp.where(
        spot < 512, (spot % SIDE) // 8, 8 + 2 * ((spot - 512) // TOK) + (spot // 8) % 2
    )

    def number_of(at):
        inside = jnp.logical_and(at >= 0, at < 128)
        return jnp.where(inside, rw_ref[jnp.clip(at, 0, 127)], -1)

    for j in range(4):
        query_number = jnp.where(
            second == 0, rw_ref[first_row + 2 * j], rw_ref[first_row + 2 * j + 1]
        )
        key_number = jnp.zeros((16, 2 * 512), jnp.int32)
        for i in range(8):
            key_number = jnp.where(key_row == i, rw_ref[first_row + i], key_number)
            rim = number_of(first_row + i + (8 if i <= 2 * j else -8))
            key_number = jnp.where(key_row == 8 + i, rim, key_number)
        bias[j] = jnp.where(key_number == query_number, 0.0, -1e30)

    own_out.wait()
    half = WIDTH // 2
    core = lax.rem(row, 2)
    mine = wo.at[pl.ds(pl.multiple_of(core * half, half), half)]
    theirs = wo.at[pl.ds(pl.multiple_of(WIDTH + core * half, half), half)]
    wo_first = remote(mine, theirs, wo_sem.at[0], wo_sem.at[1], (other + x, far_row))

    @pl.when(row == 0)
    def _():
        kv[0] = jnp.zeros((2, 8, SIDE, 2 * WIDTH), BF)

    @pl.when(row == 15)
    def _():
        kv[2] = jnp.zeros((2, 8, SIDE, 2 * WIDTH), BF)

    wave_one(0)
    for copy in loads:
        copy.wait()
    project(0, (0, x), (0, left))
    wave_two(0)
    push_own(1)
    project(0, (0, right), (0, opp))
    wave_three(0)
    project(0, (1, x), (1, left))
    wave_one(1)
    wave_four(0)
    project(0, (1, right), (1, opp))
    wo_first.wait_recv()
    wo_second = remote(theirs, theirs, wo_sem.at[2], wo_sem.at[3], (me, mate))
    project(1, (0, x), (0, left))
    wave_two(1)
    attend(0)
    project(1, (0, right), (0, opp))
    wave_three(1)
    project(1, (1, x), (1, left))
    wave_four(1)
    project(1, (1, right), (1, opp))
    wo_second.wait_recv()
    scatter_start(0)
    attend(1)
    scatter_next(0)
    scatter_start(1)
    scatter_end(0)
    scatter_next(1)
    scatter_end(1)
    for copy in sends:
        copy.wait_send()
    wo_first.wait_send()
    wo_second.wait_send()
    for c in range(2):
        for h in range(3):
            cross(c, h).wait_send()
        for direction in range(2):
            for slot in range(3):
                ring[c, direction, slot].wait_send()

    @pl.when(row < 15)
    def _():
        for c in range(2):
            for up, down in kv_copies[c]:
                up.wait_send()

    @pl.when(row > 0)
    def _():
        for c in range(2):
            for up, down in kv_copies[c]:
                down.wait_send()


def unpack_kernel(shift_ref, packed_ref, out_ref):
    packed = lax.broadcasted_iota(jnp.int32, (TOK, TOK), 1)
    rows_p, cols_p = packed_place(shift_ref[0], packed)
    pick = one_hot(lax.broadcasted_iota(jnp.int32, (TOK, TOK), 0) == rows_p * 16 + cols_p)
    out_ref[...] = jnp.dot(pick, packed_ref[...], preferred_element_type=F32).astype(BF)


VM = pl.BlockSpec(memory_space=pltpu.VMEM)
SM = pl.BlockSpec(memory_space=pltpu.SMEM)
ANY = pl.BlockSpec(memory_space=pl.ANY)
DMA = pltpu.SemaphoreType.DMA


def local(base_latent, degraded, row_window, column_shift, norm_gain, project_in, project_out):
    out = pl.pallas_call(
        layer_kernel,
        out_shape=jax.ShapeDtypeStruct((TOK, D), BF),
        in_specs=[ANY, ANY, SM, SM, VM, ANY, ANY],
        out_specs=VM,
        scratch_shapes=[
            pltpu.VMEM((TOK, D), BF),
            pltpu.VMEM((8, 8, PIECE, D), BF),
            pltpu.VMEM((8, 4, D), BF),
            pltpu.VMEM((3, D, WIDTH), BF),
            pltpu.VMEM((2 * WIDTH, D), BF),
            pltpu.VMEM((TOK, D), BF),
            pltpu.VMEM((2, 8, SIDE, WIDTH), BF),
            pltpu.VMEM((4, 2, 8, SIDE, 2 * WIDTH), BF),
            pltpu.VMEM((2, 3, 8, SIDE, HEAD), BF),
            pltpu.VMEM((2, 3, 4, SIDE, HEAD), BF),
            pltpu.VMEM((2, 4, 2, QTR, D), BF),
            pltpu.VMEM((2, 2, 3, QTR, D), BF),
            pltpu.VMEM((4, 16, 2 * 512), F32),
            DMA((2, 8)),
            DMA((2, 2, 2, 8)),
            DMA((4, 8)),
            DMA((8, 8)),
            DMA((2, 2, 8)),
            DMA((2, 2, 8)),
            DMA((5,)),
            DMA((4,)),
            DMA((2, 3)),
            DMA((2, 3)),
            DMA((2, 2, 3)),
            DMA((2, 2, 3)),
        ],
        compiler_params=pltpu.CompilerParams(
            collective_id=0, has_side_effects=True, vmem_limit_bytes=60 * 2**20
        ),
        name="layer",
    )(
        base_latent.reshape(8, 4, D),
        degraded.reshape(TOK, D),
        column_shift,
        row_window,
        norm_gain.reshape(1, D),
        project_in.transpose(1, 0, 2),
        project_out,
    )
    out = pl.pallas_call(
        unpack_kernel,
        out_shape=jax.ShapeDtypeStruct((TOK, D), BF),
        in_specs=[SM, VM],
        out_specs=VM,
        name="unpack",
    )(column_shift, out)
    return out.reshape(1, 8, 16, D)


def solution(mesh):
    placed = (
        P(None, "row", "frame", None),
        P("frame", "row", None, None),
        P(),
        P(),
        P(),
        P(None, None, "frame"),
        P("frame", None),
    )
    return jax.shard_map(
        local, mesh=mesh, in_specs=placed, out_specs=P("frame", "row", None, None), check_vma=False
    )
```

```python
import jax
import jax.numpy as jnp
from jax import lax
from jax.experimental import pallas as pl
from jax.experimental.pallas import tpu as pltpu
from jax.sharding import PartitionSpec as P

MESH = pl.DeviceIdType.MESH
HEAD = 128
D = 3072
TOK = 128
SIDE = 64
QTR = 32
WIDTH = 384
CHUNK = 768
BF = jnp.bfloat16
F32 = jnp.float32
PIECE = 16
FIRST = ((0, 1, 2), (4, 5, 6))
LATE = ((3,), (7,))
HEADING = {}
for PIECES in zip(FIRST, LATE):
    for GROUP, PLANE in ((0, 1), (0, 0), (1, 0)):
        for T in PIECES[GROUP]:
            HEADING[PLANE, T] = len(HEADING) % 2
FACTOR = HEAD ** (-0.5) * 1.4426950408889634


def packed_place(shift, token):
    column = (token // SIDE) * 8 + token % 8 + shift
    column = jnp.where(column >= 16, column - 16, column)
    return (token // 8) % 8, column


def one_hot(mask):
    return jnp.where(mask, 1.0, 0.0).astype(BF)


def layer_kernel(
    base_ref, deg_ref, shift_ref, rw_ref, gain_ref, win_ref, wout_ref,
    out_ref,
    deg, g, b, w, wo, mixed, q, kv, att, pair, part, inbox, bias,
    base_sem, x_send, z_send, g_recv, kv_send, kv_recv, w_sem, wo_sem,
    pair_send, pair_recv, part_send, part_recv,
):
    row = lax.axis_index("row")
    me = lax.axis_index("frame")
    z, x = me // 4, me % 4
    here, other = z * 4, (1 - z) * 4
    right, left, opp = lax.rem(x + 1, 4), lax.rem(x + 3, 4), lax.rem(x + 2, 4)
    mate = row + 1 - 2 * lax.rem(row, 2)
    outer = row + 2 * lax.rem(row, 2) - 1
    far_row = lax.rem(row + 8, 16)

    barrier = pltpu.get_barrier_semaphore()
    for step in range(1, 8):
        pl.semaphore_signal(
            barrier, inc=1, device_id=(lax.rem(me + step, 8), row), device_id_type=MESH
        )
    for target in ((me, mate), (other + x, far_row)):
        pl.semaphore_signal(barrier, inc=1, device_id=target, device_id_type=MESH)
    has_outer = jnp.logical_and(outer >= 0, outer < 16)

    @pl.when(has_outer)
    def _():
        pl.semaphore_signal(barrier, inc=1, device_id=(me, outer), device_id_type=MESH)

    deg_load = pltpu.make_async_copy(deg_ref, deg, w_sem.at[4])
    deg_load.start()
    loads = []
    for k in range(3):
        copy = pltpu.make_async_copy(win_ref.at[k], w.at[k], w_sem.at[k])
        copy.start()
        loads.append(copy)
    own_out = pltpu.make_async_copy(wout_ref, wo.at[pl.ds(0, WIDTH)], w_sem.at[3])
    own_out.start()

    shift = shift_ref[0]
    token = lax.broadcasted_iota(jnp.int32, (TOK, TOK), 0)
    source = lax.broadcasted_iota(jnp.int32, (TOK, TOK), 1)
    rows_q, cols_q = packed_place(shift, token)
    pick_fine = one_hot(source == rows_q * 16 + cols_q)
    deg_load.wait()
    for c in range(4):
        lanes = slice(c * CHUNK, (c + 1) * CHUNK)
        mixed[:, lanes] = jnp.dot(
            pick_fine, deg[:, lanes], preferred_element_type=F32
        ).astype(BF)

    @pl.when(has_outer)
    def _():
        pl.semaphore_wait(barrier, 10)

    @pl.when(jnp.logical_not(has_outer))
    def _():
        pl.semaphore_wait(barrier, 9)

    def remote(src, dst, send, recv, target):
        copy = pltpu.make_async_remote_copy(
            src_ref=src, dst_ref=dst, send_sem=send, recv_sem=recv,
            device_id=target, device_id_type=MESH,
        )
        copy.start()
        return copy

    base_copies = []
    for step in range(1, 8):
        to = lax.rem(me + step, 8)
        base_copies.append(
            remote(base_ref.at[to], b.at[me], base_sem.at[0, step], base_sem.at[1, step], (to, row))
        )
    own_base = pltpu.make_async_copy(base_ref.at[me], b.at[me], base_sem.at[0, 0])
    own_base.start()

    sends = []

    def item(plane, column):
        return (here if plane == 0 else other) + column

    def x_push(direction, plane, column, t, forward=0):
        frame = item(plane, column)
        to = right if direction == 0 else left
        sends.append(
            remote(g.at[frame, t], g.at[frame, t], x_send.at[direction, plane, forward, t],
                   g_recv.at[frame, t], (here + to, row))
        )

    def z_push(slot, column, t):
        frame = item(0, column)
        sends.append(
            remote(g.at[frame, t], g.at[frame, t], z_send.at[slot, t],
                   g_recv.at[frame, t], (other + x, row))
        )

    def arrive(plane, column, t):
        frame = item(plane, column)
        pltpu.make_async_remote_copy(
            src_ref=g.at[frame, t], dst_ref=g.at[frame, t], send_sem=z_send.at[0, 0],
            recv_sem=g_recv.at[frame, t], device_id=(other + x, row), device_id_type=MESH,
        ).wait_recv()

    own_base.wait()
    for copy in base_copies:
        copy.wait()
    coarse = jnp.concatenate([b[j] for j in range(8)], axis=0)

    def mix(c):
        rows = slice(c * SIDE, (c + 1) * SIDE)
        fine = lax.broadcasted_iota(jnp.int32, (SIDE, QTR), 0) + c * SIDE
        at = lax.broadcasted_iota(jnp.int32, (SIDE, QTR), 1)
        rows_c, cols_c = packed_place(shift, fine)
        pick = one_hot(at == (cols_c // 2) * 4 + rows_c // 2)
        square = jnp.zeros((SIDE, 1), F32)
        for k in range(4):
            lanes = slice(k * CHUNK, (k + 1) * CHUNK)
            up = jnp.dot(pick, coarse[:, lanes], preferred_element_type=F32)
            total = (up + mixed[rows, lanes].astype(F32)).astype(BF)
            mixed[rows, lanes] = total
            total = total.astype(F32)
            square = square + jnp.sum(total * total, axis=1, keepdims=True)
        scale = lax.rsqrt(square * (1.0 / D) + 1e-06)
        for k in range(4):
            lanes = slice(k * CHUNK, (k + 1) * CHUNK)
            normed = mixed[rows, lanes].astype(F32) * scale * gain_ref[:, lanes]
            g[me, 4 * c : 4 * c + 4, :, lanes] = normed.astype(BF).reshape(4, PIECE, CHUNK)

    def push_own(c):
        for t in FIRST[c]:
            z_push(0, x, t)
        for t in LATE[c] + FIRST[c]:
            x_push(0, 0, x, t)
            x_push(1, 0, x, t)
        for t in LATE[c]:
            z_push(0, x, t)

    def wave_one(c):
        for t in FIRST[c]:
            arrive(1, x, t)
            x_push(0, 1, x, t)
            x_push(1, 1, x, t)
        for t in LATE[c] + FIRST[c]:
            arrive(0, left, t)
            if HEADING[0, t] == 0:
                x_push(0, 0, left, t, 1)
            if t in LATE[c]:
                z_push(1, left, t)
            arrive(0, right, t)
            if HEADING[0, t] == 1:
                x_push(1, 0, right, t, 1)
            if t in LATE[c]:
                z_push(2, right, t)

    def wave_two(c):
        for t in FIRST[c]:
            arrive(1, left, t)
            if HEADING[1, t] == 0:
                x_push(0, 1, left, t, 1)
            arrive(1, right, t)
            if HEADING[1, t] == 1:
                x_push(1, 1, right, t, 1)
        for t in LATE[c]:
            arrive(0, opp, t)
            z_push(3, opp, t)
        for t in FIRST[c]:
            arrive(0, opp, t)

    def wave_three(c):
        for column in (x, left):
            for t in LATE[c]:
                arrive(1, column, t)

    def wave_four(c):
        for t in LATE[c]:
            arrive(1, right, t)
        for t in FIRST[c] + LATE[c]:
            arrive(1, opp, t)

    kv_copies = ([], [])

    def project(c, *pieces):
        frames = [item(plane, column) for plane, column in pieces]
        tokens = jnp.concatenate(
            [g[frame, 4 * c : 4 * c + 4].reshape(SIDE, D) for frame in frames], axis=0
        )
        for k in range(3):
            result = jnp.dot(tokens, w[k], preferred_element_type=F32)
            if k == 0:
                result = result * FACTOR
            result = result.astype(BF)
            for i, frame in enumerate(frames):
                value = result[i * SIDE : (i + 1) * SIDE]
                if k == 0:
                    q[c, frame] = value
                else:
                    kv[1, c, frame, :, (k - 1) * WIDTH : k * WIDTH] = value
        for frame in frames:
            n = len(kv_copies[c])
            up = pltpu.make_async_remote_copy(
                src_ref=kv.at[1, c, frame], dst_ref=kv.at[0, c, frame],
                send_sem=kv_send.at[0, c, n], recv_sem=kv_recv.at[0, c, n],
                device_id=(me, row + 1), device_id_type=MESH,
            )
            down = pltpu.make_async_remote_copy(
                src_ref=kv.at[1, c, frame], dst_ref=kv.at[2, c, frame],
                send_sem=kv_send.at[1, c, n], recv_sem=kv_recv.at[1, c, n],
                device_id=(me, row - 1), device_id_type=MESH,
            )
            kv_copies[c].append((up, down))

            @pl.when(row < 15)
            def _():
                up.start()

            @pl.when(row > 0)
            def _():
                down.start()

    def attend(c):
        @pl.when(row > 0)
        def _():
            for up, down in kv_copies[c]:
                up.wait_recv()

        @pl.when(row < 15)
        def _():
            for up, down in kv_copies[c]:
                down.wait_recv()

        even = (lax.broadcasted_iota(jnp.int32, (SIDE, 2 * WIDTH), 0) // 8) % 2 == 0

        def merge(f, carry):
            kv[3, c, f] = jnp.where(
                even, kv[2, c, f].astype(F32), kv[0, c, f].astype(F32)
            ).astype(BF)
            return carry

        lax.fori_loop(0, 8, merge, 0)
        ones = jnp.ones((2 * 512, HEAD), BF)

        def head(h, carry):
            kl = pl.ds(pl.multiple_of(h * HEAD, HEAD), HEAD)
            vl = pl.ds(pl.multiple_of(WIDTH + h * HEAD, HEAD), HEAD)
            own_key = kv[1, c, :, :, kl].reshape(512, HEAD)
            own_value = kv[1, c, :, :, vl].reshape(512, HEAD)
            for j in range(4):
                at = slice(16 * j, 16 * j + 16)
                keys, values = [own_key], [own_value]
                for p in range(4):
                    band = 2 if j > p else (3 if j == p else 0)
                    rows = slice(16 * p, 16 * p + 16)
                    keys.append(kv[band, c, :, rows, kl].reshape(TOK, HEAD))
                    values.append(kv[band, c, :, rows, vl].reshape(TOK, HEAD))
                value = jnp.concatenate([jnp.concatenate(values, axis=0), ones], axis=1)
                scores = lax.dot_general(
                    q[c, :, at, kl].reshape(TOK, HEAD), jnp.concatenate(keys, axis=0),
                    (((1,), (1,)), ((), ())), preferred_element_type=F32,
                )
                scores = (scores.reshape(8, 16, 2 * 512) + bias[j][None]).reshape(TOK, 2 * 512)
                raised = jnp.exp2(scores - jnp.max(scores, axis=1, keepdims=True))
                result = jnp.dot(raised.astype(BF), value, preferred_element_type=F32)
                result = result[:, :HEAD] / result[:, HEAD:]
                att[c, h, :, at, :] = result.astype(BF).reshape(8, 16, HEAD)
            cross(c, h).start()
            return carry

        lax.fori_loop(0, 3, head, 0)

    def cross(c, h):
        return pltpu.make_async_remote_copy(
            src_ref=att.at[c, h, pl.ds(other, 4)], dst_ref=pair.at[c, h],
            send_sem=pair_send.at[c, h], recv_sem=pair_recv.at[c, h],
            device_id=(other + x, row), device_id_type=MESH,
        )

    order = (opp, right, left, x)

    def multiply(c, first):
        halves = []
        for k in (first, first + 1):
            heads = [att[c, h, here + order[k]] for h in range(3)]
            heads += [pair[c, h, order[k]] for h in range(3)]
            halves.append(jnp.concatenate(heads, axis=1))
        tokens = jnp.concatenate(halves, axis=0)
        for n in range(4):
            lanes = slice(n * CHUNK, (n + 1) * CHUNK)
            part[c, first : first + 2, :, :, lanes] = (
                jnp.dot(tokens, wo[:, lanes], preferred_element_type=F32)
                .astype(BF)
                .reshape(2, 2, QTR, CHUNK)
            )

    ring = {}

    def push(c, direction, slot, k, h):
        to = right if direction == 0 else left
        ring[c, direction, slot] = remote(
            part.at[c, k, h], inbox.at[c, direction, slot], part_send.at[c, direction, slot],
            part_recv.at[c, direction, slot], (here + to, row),
        )

    def scatter_start(c):
        for h in range(3):
            cross(c, h).wait_recv()
        multiply(c, 0)
        push(c, 0, 0, 0, 0)
        push(c, 1, 0, 0, 1)
        push(c, 0, 1, 1, 1)
        multiply(c, 2)
        push(c, 1, 1, 2, 0)

    def scatter_next(c):
        ring[c, 0, 0].wait_recv()
        part[c, 1, 0] = (part[c, 1, 0].astype(F32) + inbox[c, 0, 0].astype(F32)).astype(BF)
        push(c, 0, 2, 1, 0)
        ring[c, 1, 0].wait_recv()
        part[c, 2, 1] = (part[c, 2, 1].astype(F32) + inbox[c, 1, 0].astype(F32)).astype(BF)
        push(c, 1, 2, 2, 1)

    def scatter_end(c):
        for direction in range(2):
            for slot in (1, 2):
                ring[c, direction, slot].wait_recv()
        for h in range(2):
            rows = slice(c * SIDE + h * QTR, c * SIDE + (h + 1) * QTR)
            total = part[c, 3, h].astype(F32) + inbox[c, 0, 2 - h].astype(F32)
            total = total + inbox[c, 1, 1 + h].astype(F32)
            out_ref[rows, :] = (total + mixed[rows, :].astype(F32)).astype(BF)

    mix(0)
    push_own(0)
    mix(1)

    first_row = row * 8
    spot = lax.broadcasted_iota(jnp.int32, (16, 2 * 512), 1)
    second = lax.broadcasted_iota(jnp.int32, (16, 2 * 512), 0) // 8
    key_row = jnp.where(
        spot < 512, (spot % SIDE) // 8, 8 + 2 * ((spot - 512) // TOK) + (spot // 8) % 2
    )

    def number_of(at):
        inside = jnp.logical_and(at >= 0, at < 128)
        return jnp.where(inside, rw_ref[jnp.clip(at, 0, 127)], -1)

    for j in range(4):
        query_number = jnp.where(
            second == 0, rw_ref[first_row + 2 * j], rw_ref[first_row + 2 * j + 1]
        )
        key_number = jnp.zeros((16, 2 * 512), jnp.int32)
        for i in range(8):
            key_number = jnp.where(key_row == i, rw_ref[first_row + i], key_number)
            rim = number_of(first_row + i + (8 if i <= 2 * j else -8))
            key_number = jnp.where(key_row == 8 + i, rim, key_number)
        bias[j] = jnp.where(key_number == query_number, 0.0, -1e30)

    own_out.wait()
    half = WIDTH // 2
    core = lax.rem(row, 2)
    mine = wo.at[pl.ds(pl.multiple_of(core * half, half), half)]
    theirs = wo.at[pl.ds(pl.multiple_of(WIDTH + core * half, half), half)]
    wo_first = remote(mine, theirs, wo_sem.at[0], wo_sem.at[1], (other + x, far_row))

    @pl.when(row == 0)
    def _():
        kv[0] = jnp.zeros((2, 8, SIDE, 2 * WIDTH), BF)

    @pl.when(row == 15)
    def _():
        kv[2] = jnp.zeros((2, 8, SIDE, 2 * WIDTH), BF)

    wave_one(0)
    for copy in loads:
        copy.wait()
    project(0, (0, x), (0, left))
    wave_two(0)
    project(0, (0, right), (0, opp))
    push_own(1)
    wave_three(0)
    project(0, (1, x), (1, left))
    wave_one(1)
    wave_four(0)
    project(0, (1, right), (1, opp))
    wo_first.wait_recv()
    wo_second = remote(theirs, theirs, wo_sem.at[2], wo_sem.at[3], (me, mate))
    project(1, (0, x), (0, left))
    wave_two(1)
    attend(0)
    project(1, (0, right), (0, opp))
    wave_three(1)
    project(1, (1, x), (1, left))
    wave_four(1)
    project(1, (1, right), (1, opp))
    wo_second.wait_recv()
    scatter_start(0)
    attend(1)
    scatter_next(0)
    scatter_start(1)
    scatter_end(0)
    scatter_next(1)
    scatter_end(1)
    for copy in sends:
        copy.wait_send()
    wo_first.wait_send()
    wo_second.wait_send()
    for c in range(2):
        for h in range(3):
            cross(c, h).wait_send()
        for direction in range(2):
            for slot in range(3):
                ring[c, direction, slot].wait_send()

    @pl.when(row < 15)
    def _():
        for c in range(2):
            for up, down in kv_copies[c]:
                up.wait_send()

    @pl.when(row > 0)
    def _():
        for c in range(2):
            for up, down in kv_copies[c]:
                down.wait_send()


def unpack_kernel(shift_ref, packed_ref, out_ref):
    packed = lax.broadcasted_iota(jnp.int32, (TOK, TOK), 1)
    rows_p, cols_p = packed_place(shift_ref[0], packed)
    pick = one_hot(lax.broadcasted_iota(jnp.int32, (TOK, TOK), 0) == rows_p * 16 + cols_p)
    out_ref[...] = jnp.dot(pick, packed_ref[...], preferred_element_type=F32).astype(BF)


VM = pl.BlockSpec(memory_space=pltpu.VMEM)
SM = pl.BlockSpec(memory_space=pltpu.SMEM)
ANY = pl.BlockSpec(memory_space=pl.ANY)
DMA = pltpu.SemaphoreType.DMA


def local(base_latent, degraded, row_window, column_shift, norm_gain, project_in, project_out):
    out = pl.pallas_call(
        layer_kernel,
        out_shape=jax.ShapeDtypeStruct((TOK, D), BF),
        in_specs=[ANY, ANY, SM, SM, VM, ANY, ANY],
        out_specs=VM,
        scratch_shapes=[
            pltpu.VMEM((TOK, D), BF),
            pltpu.VMEM((8, 8, PIECE, D), BF),
            pltpu.VMEM((8, 4, D), BF),
            pltpu.VMEM((3, D, WIDTH), BF),
            pltpu.VMEM((2 * WIDTH, D), BF),
            pltpu.VMEM((TOK, D), BF),
            pltpu.VMEM((2, 8, SIDE, WIDTH), BF),
            pltpu.VMEM((4, 2, 8, SIDE, 2 * WIDTH), BF),
            pltpu.VMEM((2, 3, 8, SIDE, HEAD), BF),
            pltpu.VMEM((2, 3, 4, SIDE, HEAD), BF),
            pltpu.VMEM((2, 4, 2, QTR, D), BF),
            pltpu.VMEM((2, 2, 3, QTR, D), BF),
            pltpu.VMEM((4, 16, 2 * 512), F32),
            DMA((2, 8)),
            DMA((2, 2, 2, 8)),
            DMA((4, 8)),
            DMA((8, 8)),
            DMA((2, 2, 8)),
            DMA((2, 2, 8)),
            DMA((5,)),
            DMA((4,)),
            DMA((2, 3)),
            DMA((2, 3)),
            DMA((2, 2, 3)),
            DMA((2, 2, 3)),
        ],
        compiler_params=pltpu.CompilerParams(
            collective_id=0, has_side_effects=True, vmem_limit_bytes=60 * 2**20
        ),
        name="layer",
    )(
        base_latent.reshape(8, 4, D),
        degraded.reshape(TOK, D),
        column_shift,
        row_window,
        norm_gain.reshape(1, D),
        project_in.transpose(1, 0, 2),
        project_out,
    )
    out = pl.pallas_call(
        unpack_kernel,
        out_shape=jax.ShapeDtypeStruct((TOK, D), BF),
        in_specs=[SM, VM],
        out_specs=VM,
        name="unpack",
    )(column_shift, out)
    return out.reshape(1, 8, 16, D)


def solution(mesh):
    placed = (
        P(None, "row", "frame", None),
        P("frame", "row", None, None),
        P(),
        P(),
        P(),
        P(None, None, "frame"),
        P("frame", None),
    )
    return jax.shard_map(
        local, mesh=mesh, in_specs=placed, out_specs=P("frame", "row", None, None), check_vma=False
    )
```
